32 devices in a mesh: ox: 4 (over z), oy: 8 (over y, x, core).
Axes of the slice: x: 2, y: 2, z: 4, core: 2. Of those that a mesh axis runs over, the one named last changes fastest.
Arguments:
- zonal_flow: float32 [4, 512, 1024], P(None, 'ox', 'oy'), may hold values from -3 to 3
- merid_flow: float32 [4, 512, 1024], P(None, 'ox', 'oy'), may hold values from -3 to 3
- thickness: float32 [4, 512, 1024], P(None, 'ox', 'oy'), may hold values from 0.8 to 2
- land_sea: int32 [512, 1024], P('ox', 'oy'), may hold values 0 or 1
- viscosity: float32 [512, 1024], P('ox', 'oy'), may hold values from 0.2 to 3
- wind_stress: float32 [2, 512, 1024], P(None, 'ox', 'oy'), may hold values from -5 to 5
- reduced_gravity: float32 [4], replicated, may hold values from 0.1 to 1
- conv_first: bfloat16 [3, 3, 64, 4], replicated, may hold values from -1 to 1
- bias_first: float32 [64], replicated, may hold values from -3 to 3
- conv_second: bfloat16 [3, 3, 64, 64], replicated, may hold values from -0.25 to 0.25
- bias_second: float32 [64], replicated, may hold values from -3 to 3
- conv_last: bfloat16 [3, 3, 1, 64], replicated, may hold values from -0.25 to 0.25
Outputs:
- zonal_next: float32 [4, 512, 1024], P(None, 'ox', 'oy')
- merid_next: float32 [4, 512, 1024], P(None, 'ox', 'oy')
- thickness_next: float32 [4, 512, 1024], P(None, 'ox', 'oy')
- viscosity_next: float32 [512, 1024], P('ox', 'oy')
The draws below stay inside these ranges and needn't reach their ends.
Inputs may be any that keep to these rules, and one draw needn't show every extreme that they name: `land_sea`: 1 marks a sea cell.
All inputs are finite; a program needn't handle non-finite values. No bound on the sum of `land_sea` on one device may be relied on, other than what follows from the above.
Results may differ from the reference program's by a relative error of at most 0.0019.
Values may be sent and summed in bfloat16 or wider, within the bound.
No kernel may reach another device: no remote copies, remote signals or barrier semaphores. Data moves between devices by JAX's collectives and lax.ppermute only.
A program may use at most 192 MiB of HBM per device.

```python
import math
import jax
import jax.numpy as jnp
from jax import lax

CX = 128
LAYERS = 4
FEATURES = 4
HIDDEN_SIZE = 64
NX = 512
NY = 1024


def with_ends(entries, key, low, largest):
    place = [jax.random.randint(jax.random.fold_in(key, axis), (), 0, length) for axis, length in enumerate(entries.shape)]
    widest = entries.shape.index(max(entries.shape))
    neighbour = place[:widest] + [(place[widest] + 1) % entries.shape[widest]] + place[widest + 1:]
    return entries.at[tuple(place)].set(low).at[tuple(neighbour)].set(largest)


def block_scale(own_key, dims, split, low, top_value):
    loudness, own = 1.0, jax.random.fold_in(own_key, 6)
    for position, shards_of in split:
        steps = jnp.exp(jax.random.uniform(jax.random.fold_in(own, position), (shards_of,), jnp.float32, low / len(split), top_value / len(split)))
        loudness = loudness * jnp.repeat(steps, dims[position] // shards_of).reshape([-1 if axis == position else 1 for axis in range(len(dims))])
    return loudness


def scatter_about(rng, dims, scale, most, pieces=(), held_as=jnp.bfloat16):
    loudness = block_scale(rng, dims, pieces, -0.22, 0.18) if pieces else 1.0
    entries = jax.random.normal(rng, dims, jnp.float32) * scale * loudness
    return jnp.minimum(jnp.maximum(entries, -most), most).astype(held_as)


def setup_inputs(seed: int = 0) -> dict:
    splits = jax.random.split(jax.random.key(seed), 13)
    zonal_flow = scatter_about(splits[0], (LAYERS, NX, NY), 0.5, 3.0, ((1, 4), (2, 8)), jnp.float32)
    merid_flow = scatter_about(splits[1], (LAYERS, NX, NY), 0.5, 3.0, ((1, 4), (2, 8)), jnp.float32)
    thickness = jnp.clip(0.8 + 1.2 * jax.random.uniform(splits[2], (LAYERS, NX, NY), jnp.float32) ** block_scale(splits[2], (LAYERS, NX, NY), ((1, 4), (2, 8)), -0.2, 0.2), 0.8, 2.0)
    land_sea = with_ends((jax.random.randint(splits[3], (NX, NY), 0, 5) < 4).astype(jnp.int32), jax.random.fold_in(splits[3], 1), 0, 1)
    viscosity = jnp.clip(jnp.exp(math.log(3.0) - 2.7080502 * jax.random.uniform(splits[4], (NX, NY), jnp.float32) ** block_scale(splits[4], (NX, NY), ((0, 4), (1, 8)), -0.2, 0.2)), 0.2, 3.0)
    wind_stress = scatter_about(splits[5], (2, NX, NY), 1.0, 5.0, ((1, 4), (2, 8)), jnp.float32)
    reduced_gravity = jnp.clip(jnp.exp(jax.random.uniform(splits[6], (LAYERS,), jnp.float32, math.log(0.1), math.log(1.0))), 0.1, 1.0)
    conv_first = scatter_about(splits[7], (3, 3, HIDDEN_SIZE, FEATURES), (9 * FEATURES) ** -0.5, 1.0)
    bias_first = scatter_about(splits[8], (HIDDEN_SIZE,), 0.5, 3.0, (), jnp.float32)
    conv_second = scatter_about(splits[9], (3, 3, HIDDEN_SIZE, HIDDEN_SIZE), (9 * HIDDEN_SIZE) ** -0.5, 0.25)
    bias_second = scatter_about(splits[10], (HIDDEN_SIZE,), 0.5, 3.0, (), jnp.float32)
    conv_last = scatter_about(splits[11], (3, 3, 1, HIDDEN_SIZE), (9 * HIDDEN_SIZE) ** -0.5, 0.25)
    return dict(zonal_flow=zonal_flow, merid_flow=merid_flow, thickness=thickness, land_sea=land_sea, viscosity=viscosity, wind_stress=wind_stress, reduced_gravity=reduced_gravity, conv_first=conv_first, bias_first=bias_first, conv_second=conv_second, bias_second=bias_second, conv_last=conv_last)


TIME_STEP = 0.05
REST_DEPTH = 1.4
DRAG_RATE = 0.5


def neighbours(field):
    east = jnp.roll(field, -1, axis=-2)
    west = jnp.roll(field, 1, axis=-2)
    zeros = jnp.zeros_like(field[..., :1])
    north = jnp.concatenate([field[..., 1:], zeros], axis=-1)
    south = jnp.concatenate([zeros, field[..., :-1]], axis=-1)
    return east, west, north, south


def viscous(field, near, visc, visc_near):
    total = 0.5 * (visc + visc_near[0]) * (near[0] - field)
    for side in range(1, 4):
        total = total + 0.5 * (visc + visc_near[side]) * (near[side] - field)
    return total


def conv_valid(extended, weight):
    width = extended.shape[1] - 2
    height = extended.shape[2] - 2
    total = jnp.zeros((weight.shape[2], width, height), jnp.float32)
    for row_off in range(3):
        for col_off in range(3):
            total = total + jnp.einsum("oc,cxy->oxy", weight[row_off, col_off].astype(jnp.float32),
                                       extended[:, row_off:row_off + width, col_off:col_off + height])
    return total


def pad_lat(field):
    return jnp.pad(field, ((0, 0), (0, 0), (1, 1)))


def reference(zonal_flow, merid_flow, thickness, land_sea, viscosity, wind_stress, reduced_gravity,
              conv_first, bias_first, conv_second, bias_second, conv_last):
    sea = land_sea.astype(jnp.float32)
    zonal_m = zonal_flow * sea
    merid_m = merid_flow * sea
    flux_x = zonal_m * thickness
    flux_y = merid_m * thickness
    flux_e, flux_w, unused_n, unused_s = neighbours(flux_x)
    unused_e, unused_w, flux_n, flux_s = neighbours(flux_y)
    diverge = (flux_e - flux_w) * 0.5 + (flux_n - flux_s) * 0.5
    thickness_next = thickness - TIME_STEP * sea * diverge
    anomaly = thickness_next - REST_DEPTH
    interface = jnp.cumsum(anomaly[::-1], axis=0)[::-1]
    pressure = jnp.cumsum(reduced_gravity[:, None, None] * interface, axis=0)
    press_e, press_w, press_n, press_s = neighbours(pressure)
    grad_x = (press_e - press_w) * 0.5
    grad_y = (press_n - press_s) * 0.5
    visc_near = neighbours(viscosity)
    zonal_visc = viscous(zonal_m, neighbours(zonal_m), viscosity, visc_near)
    merid_visc = viscous(merid_m, neighbours(merid_m), viscosity, visc_near)
    lat_rows = jnp.arange(NY).astype(jnp.float32)
    coriolis = 0.3 + 1.4 * (lat_rows + 0.5) / NY
    layer_ids = jnp.arange(LAYERS)
    top = (layer_ids == 0).astype(jnp.float32)[:, None, None]
    bottom = (layer_ids == LAYERS - 1).astype(jnp.float32)[:, None, None]
    force_x = wind_stress[0] / thickness_next[0]
    force_y = wind_stress[1] / thickness_next[0]
    zonal_next = sea * (zonal_m + TIME_STEP * (coriolis * merid_m - grad_x + zonal_visc + top * force_x
                                               - DRAG_RATE * bottom * zonal_m))
    merid_next = sea * (merid_m + TIME_STEP * (-coriolis * zonal_m - grad_y + merid_visc + top * force_y
                                               - DRAG_RATE * bottom * merid_m))
    energy = 0.5 * jnp.sum(thickness_next * (zonal_next * zonal_next + merid_next * merid_next), axis=0)
    energy = energy / jnp.sum(thickness_next, axis=0)
    features = jnp.stack([zonal_next[0], merid_next[0], sea * (thickness_next[0] - REST_DEPTH),
                          sea * energy]).astype(jnp.bfloat16)

    def net_block(block):
        columns = ((block * CX - 3 + jnp.arange(CX + 6)) % NX).astype(jnp.int32)
        hidden = jnp.take(features, columns, axis=1).astype(jnp.float32)
        for weight, bias_term in ((conv_first, bias_first), (conv_second, bias_second)):
            summed = conv_valid(pad_lat(hidden), weight) + bias_term[:, None, None]
            rounded = jax.nn.silu(summed).astype(jnp.bfloat16)
            hidden = lax.optimization_barrier(rounded).astype(jnp.float32)
        output = conv_valid(pad_lat(hidden), conv_last)
        return jnp.exp(output[0])

    blocks = lax.map(net_block, jnp.arange(NX // CX).astype(jnp.int32))
    viscosity_next = blocks.reshape(NX, NY)
    return zonal_next, merid_next, thickness_next, viscosity_next
```

```python
import functools

import jax
import jax.numpy as jnp
from jax import lax
from jax.experimental import pallas as pl
from jax.experimental.pallas import tpu as pltpu
from jax.sharding import PartitionSpec as P

TIME_STEP = 0.05
REST_DEPTH = 1.4
DRAG_RATE = 0.5

F32 = jnp.float32
BF16 = jnp.bfloat16
EDGE = 8
FIELDS = 16
PITCH = 80
VMEM = pl.BlockSpec(memory_space=pltpu.VMEM)


def own_fields(zonal, merid, thick, land, visc, wind, rows):
    sea = land[rows, :].astype(F32)
    layers = zonal.shape[0]
    maps = [zonal[l, rows, :] * sea for l in range(layers)]
    maps += [merid[l, rows, :] * sea for l in range(layers)]
    maps += [thick[l, rows, :] - REST_DEPTH for l in range(layers)]
    return maps + [sea, visc[rows, :], wind[0, rows, :], wind[1, rows, :]]


def pack_kernel(zonal, merid, thick, land, visc, wind, lat_a, lat_b, lon_a, lon_b):
    columns, lat = land.shape
    even_y = lax.rem(lax.axis_index("oy"), 2) == 0
    even_x = lax.rem(lax.axis_index("ox"), 2) == 0
    lane = lax.broadcasted_iota(jnp.int32, (16, lat), 1) // EDGE
    maps_low = own_fields(zonal, merid, thick, land, visc, wind, slice(0, EDGE))
    maps_high = own_fields(zonal, merid, thick, land, visc, wind, slice(columns - EDGE, columns))
    for f in range(0, FIELDS, 2):
        low = jnp.concatenate(maps_low[f : f + 2], axis=0)
        high = jnp.concatenate(maps_high[f : f + 2], axis=0)
        lon_a[EDGE * f : EDGE * f + 16, :] = jnp.where(even_x, high, low).astype(BF16)
        lon_b[EDGE * f : EDGE * f + 16, :] = jnp.where(even_x, low, high).astype(BF16)
    for c in range(0, columns, 16):
        low = jnp.zeros((16, lat), F32)
        high = jnp.zeros((16, lat), F32)
        for f, field in enumerate(own_fields(zonal, merid, thick, land, visc, wind, slice(c, c + 16))):
            here = lane == f
            low = jnp.where(here, pltpu.roll(field, EDGE * f % lat, 1), low)
            high = jnp.where(here, pltpu.roll(field, (EDGE * f + EDGE) % lat, 1), high)
        lat_a[c : c + 16, :] = jnp.where(even_y, high, low).astype(BF16)
        lat_b[c : c + 16, :] = jnp.where(even_y, low, high).astype(BF16)


def corner_kernel(lon_a, lon_b, got_a, got_b, out_a, out_b):
    columns = got_a.shape[0]
    even_x = lax.rem(lax.axis_index("ox"), 2) == 0
    size = lon_a.shape[0]
    out_a[0:size, :] = lon_a[...]
    out_b[0:size, :] = lon_b[...]
    for n, got in enumerate((got_a, got_b)):
        low = got[0:16, :]
        high = got[columns - 16 : columns, :]
        out_a[size + 16 * n : size + 16 * n + 16, :] = jnp.where(even_x, high, low)
        out_b[size + 16 * n : size + 16 * n + 16, :] = jnp.where(even_x, low, high)


def weight_kernel(first, second, last, bias_first, bias_second, w1, w2, w3, b1, b2):
    hidden = second.shape[2]
    zero = jnp.zeros((hidden, hidden), F32)
    turned = [[second[a, b].astype(F32).T * 0.5 for b in range(3)] for a in range(3)]
    tap = lambda a, b: turned[a][b] if 0 <= a < 3 and 0 <= b < 3 else zero
    for px in range(4):
        for py in range(4):
            ex, ey, a, b = px % 2, py % 2, px // 2, py // 2
            row = ((2 * a + b) * 4 + 2 * ex + ey) * hidden
            for dx in range(2):
                w2[row : row + hidden, 128 * dx : 128 * dx + 128] = jnp.concatenate(
                    [tap(px - dx, py), tap(px - dx, py - 1)], axis=1
                ).astype(BF16)
    feats = first.shape[3]
    spot = lax.broadcasted_iota(jnp.int32, (256, feats), 0)
    chan = lax.broadcasted_iota(jnp.int32, (256, feats), 1)
    total = jnp.zeros((256, hidden), F32)
    ddx, ddy = spot // 128, (spot // 64) % 2
    for a in range(3):
        for b in range(3):
            want = ((ddx + a) * 4 + ddy + b) * feats + chan
            place = jnp.where(spot % 64 == want, 0.5, 0.0).astype(BF16)
            total = total + lax.dot_general(
                place, first[a, b], (((1,), (1,)), ((), ())), preferred_element_type=F32
            )
    base = jnp.concatenate(
        [
            jnp.concatenate([total[0:64], total[64:128]], axis=1),
            jnp.concatenate([total[128:192], total[192:256]], axis=1),
        ],
        axis=1,
    )
    for s in range(4):
        off = 80 + 32 * s
        w1[s] = jnp.concatenate(
            [jnp.zeros((off, 256), F32), base, jnp.zeros((192 - off, 256), F32)], axis=0
        ).astype(BF16)
    row = lax.broadcasted_iota(jnp.int32, (16, 128), 0)
    blank = jnp.zeros((1, hidden), F32)
    piece = lambda a, b: last[a, b].astype(F32) if 0 <= a < 3 and 0 <= b < 3 else blank
    for ex in range(2):
        tile = jnp.zeros((16, 128), F32)
        for k in range(16):
            a, dx, b, dy = k // 8, (k // 4) % 2, (k // 2) % 2, k % 2
            p, q = 2 * a + ex - dx, 2 * b - dy
            line = jnp.concatenate([piece(p, q), piece(p, q + 1)], axis=1)
            tile = jnp.where(row == k, jnp.broadcast_to(line, (16, 128)), tile)
        w3[:, 128 * ex : 128 * ex + 128] = tile.astype(BF16)
    for bias, out in ((bias_first, b1), (bias_second, b2)):
        half = bias[...] * 0.5
        out[...] = jnp.broadcast_to(jnp.concatenate([half] * 4, axis=1), (8, 256))


def main_kernel(
    lat_count,
    zonal,
    merid,
    thick,
    land,
    visc,
    wind,
    gravity,
    lat_a,
    lat_b,
    lon_a,
    lon_b,
    w1,
    w2,
    w3,
    b1,
    b2,
    zonal_out,
    merid_out,
    thick_out,
    visc_out,
    ext,
    nxt,
    prs,
    spread,
    feat,
    act,
    act_up,
    parts,
    sums,
):
    layers, columns, lat = zonal.shape
    oy = lax.axis_index("oy")
    even_y = lax.rem(oy, 2) == 0
    even_x = lax.rem(lax.axis_index("ox"), 2) == 0
    base = 2 * EDGE
    wide = 2 * lat
    sea_id, visc_id, wind_id = 3 * layers, 3 * layers + 1, 3 * layers + 2

    west = jnp.where(even_x, lon_b[...], lon_a[...])
    east = jnp.where(even_x, lon_a[...], lon_b[...])
    size = EDGE * FIELDS
    north, south = [], []
    for side, slot in ((west, slice(8, 16)), (east, slice(0, 8))):
        from_a = side[size : size + 16].astype(F32)[slot]
        from_b = side[size + 16 : size + 32].astype(F32)[slot]
        north.append(jnp.where(even_y, from_a, from_b))
        south.append(jnp.where(even_y, from_b, from_a))
    west = west[:size].astype(F32)
    east = east[:size].astype(F32)
    lane = lax.broadcasted_iota(jnp.int32, (EDGE, lat), 1)

    def second_tile(n_rows, s_rows, f):
        up = pltpu.roll(n_rows, (lat - EDGE * f) % lat, 1)
        down = pltpu.roll(s_rows, (2 * lat - EDGE - EDGE * f) % lat, 1)
        return jnp.where(lane < EDGE, up, jnp.where(lane >= lat - EDGE, down, 0.0))

    def put(f, row, first_tile, n_rows, s_rows):
        far = second_tile(n_rows, s_rows, f)
        if 2 * layers <= f < 3 * layers:
            far = far + REST_DEPTH
        ext[f, row : row + EDGE, 0:lat] = first_tile
        ext[f, row : row + EDGE, lat:wide] = far

    for f in range(FIELDS):
        lift = REST_DEPTH if 2 * layers <= f < 3 * layers else 0.0
        put(f, base - EDGE, west[EDGE * f : EDGE * f + EDGE] + lift, north[0], south[0])
        put(f, base + columns, east[EDGE * f : EDGE * f + EDGE] + lift, north[1], south[1])
    for c in range(0, columns, 16):
        got_a = lat_a[c : c + 16, :].astype(F32)
        got_b = lat_b[c : c + 16, :].astype(F32)
        n_both = jnp.where(even_y, got_a, got_b)
        s_both = jnp.where(even_y, got_b, got_a)
        for h in range(0, 16, EDGE):
            rows = slice(c + h, c + h + EDGE)
            sea = land[rows, :].astype(F32)
            maps = [zonal[l, rows, :] * sea for l in range(layers)]
            maps += [merid[l, rows, :] * sea for l in range(layers)]
            maps += [thick[l, rows, :] for l in range(layers)]
            maps += [sea, visc[rows, :], wind[0, rows, :], wind[1, rows, :]]
            for f in range(FIELDS):
                put(f, base + c + h, maps[f], n_both[h : h + EDGE], s_both[h : h + EDGE])

    def up(x):
        return pltpu.roll(x, wide - 1, 1)

    def down(x):
        return pltpu.roll(x, 1, 1)

    chunks = (columns + 2 * EDGE) // EDGE
    for ch in range(chunks):
        r = EDGE + EDGE * ch
        here, plus, minus = slice(r, r + 8), slice(r + 1, r + 9), slice(r - 1, r + 7)
        sea = ext[sea_id, here, :]
        odd = []
        for l in range(layers):
            h = ext[2 * layers + l, here, :]
            flux_e = ext[l, plus, :] * ext[2 * layers + l, plus, :]
            flux_w = ext[l, minus, :] * ext[2 * layers + l, minus, :]
            flux_y = ext[layers + l, here, :] * h
            diverge = (flux_e - flux_w) * 0.5 + (up(flux_y) - down(flux_y)) * 0.5
            h = h - TIME_STEP * sea * diverge
            nxt[l, r : r + 8, :] = h
            if 1 <= ch < chunks - 1:
                thick_out[l, r - base : r - base + 8, :] = h[:, 0:lat]
            odd.append(h - REST_DEPTH)
        for l in reversed(range(layers - 1)):
            odd[l] = odd[l] + odd[l + 1]
        total = jnp.zeros_like(sea)
        for l in range(layers):
            total = total + gravity[l] * odd[l]
            prs[l, r : r + 8, :] = total

    place = lax.broadcasted_iota(jnp.int32, (EDGE, wide), 1)
    place = jnp.where(place < lat + lat // 2, place, place - wide)
    total_rows = lat_count * lat
    coriolis = 0.3 + 1.4 * ((oy * lat + place).astype(F32) + 0.5) / total_rows
    in_lat = (place >= -3) & (place < lat + 3)
    for ch in range(chunks):
        r = EDGE + EDGE * ch
        here, plus, minus = slice(r, r + 8), slice(r + 1, r + 9), slice(r - 1, r + 7)
        sea = ext[sea_id, here, :]
        v = ext[visc_id, here, :]
        mix = [
            0.5 * (v + ext[visc_id, plus, :]),
            0.5 * (v + ext[visc_id, minus, :]),
            0.5 * (v + up(v)),
            0.5 * (v + down(v)),
        ]

        def lap(f, q):
            near = (ext[f, plus, :], ext[f, minus, :], up(q), down(q))
            total = mix[0] * (near[0] - q)
            for side in range(1, 4):
                total = total + mix[side] * (near[side] - q)
            return total

        heavy = jnp.zeros_like(sea)
        moving = jnp.zeros_like(sea)
        for l in range(layers):
            zm = ext[l, here, :]
            vm = ext[layers + l, here, :]
            p = prs[l, here, :]
            h = nxt[l, here, :]
            grad_x = (prs[l, plus, :] - prs[l, minus, :]) * 0.5
            grad_y = (up(p) - down(p)) * 0.5
            push_x = coriolis * vm - grad_x + lap(l, zm)
            push_y = -coriolis * zm - grad_y + lap(layers + l, vm)
            if l == 0:
                push_x = push_x + ext[wind_id, here, :] / h
                push_y = push_y + ext[wind_id + 1, here, :] / h
            if l == layers - 1:
                push_x = push_x - DRAG_RATE * zm
                push_y = push_y - DRAG_RATE * vm
            zn = sea * (zm + TIME_STEP * push_x)
            vn = sea * (vm + TIME_STEP * push_y)
            if 1 <= ch < chunks - 1:
                zonal_out[l, r - base : r - base + 8, :] = zn[:, 0:lat]
                merid_out[l, r - base : r - base + 8, :] = vn[:, 0:lat]
            heavy = heavy + h
            moving = moving + h * (zn * zn + vn * vn)
            if l == 0:
                maps = [zn, vn, sea * (h - REST_DEPTH)]
        maps.append(sea * (0.5 * moving / heavy))
        keep = in_lat
        if ch == 0 or ch == chunks - 1:
            column = lax.broadcasted_iota(jnp.int32, (EDGE, wide), 0) + (r - base)
            keep = keep & (column >= -3) & (column < columns + 3)
        for f, m in enumerate(maps):
            m = jnp.where(keep, m, 0.0)
            for dy in range(4):
                spread[EDGE * ch : EDGE * ch + 8, 4 * dy + f, :] = pltpu.roll(m, (wide - dy) % wide, 1) if dy else m

    block = lax.broadcasted_iota(jnp.int32, (PITCH, wide), 0)
    source = lax.broadcasted_iota(jnp.int32, (PITCH, wide), 1)
    blocks = lat // 2 + 2
    chooser = jnp.where(
        (block < blocks) & (source == lax.rem(wide - 3 + 2 * block, wide)), 1.0, 0.0
    ).astype(BF16)
    tiles = (columns + 2 * EDGE) // 8
    for t in range(0, tiles, 2):
        got = spread[8 * t : 8 * t + 16].reshape(256, wide).astype(BF16)
        g = lax.dot_general(
            chooser, got, (((1,), (1,)), ((), ())), preferred_element_type=F32
        ).astype(BF16)
        feat[t, :, 0:128] = g[:, 0:128]
        feat[t, :, 128:256] = g[:, 128:256]
        feat[t + 1, :, 0:128] = g[:, 128:256]
        if t > 0:
            feat[t - 1, :, 128:256] = g[:, 0:128]

    south_end = jnp.where(oy == 0, 0.0, 1.0)
    north_end = jnp.where(oy == lat_count - 1, 0.0, 1.0)
    brow = lax.broadcasted_iota(jnp.int32, (8, 256), 0)
    quad = lax.broadcasted_iota(jnp.int32, (8, 256), 1) // 64 % 2
    low_1 = jnp.where(brow == 0, south_end, 1.0)
    high_1 = jnp.where(brow == blocks - 1 - 64, north_end, 1.0)
    low_2 = jnp.where((brow == 0) & (quad == 0), south_end, 1.0)
    high_2 = jnp.where((brow == blocks - 2 - 64) & (quad == 1), north_end, 1.0)

    def activate(total, bias, count, low, high):
        total = total + bias
        total = total * jnp.tanh(total) + total
        total = total.reshape(count, PITCH, 256)
        return jnp.concatenate(
            [total[:, 0:8] * low, total[:, 8:64], total[:, 64:72] * high, total[:, 72:]], axis=1
        )

    bias1 = b1[0:1, :]
    bias2 = b2[0:1, :]
    group = 4

    def first_conv(t, count, s):
        left = feat[pl.ds(t, count)].reshape(count * PITCH, 256)
        h = jnp.dot(left, w1[s], preferred_element_type=F32)
        h = activate(h, bias1, count, low_1, high_1)
        flat = h.reshape(count * PITCH, 256)
        moved = pltpu.roll(flat, count * PITCH - 1, 0).reshape(count, PITCH, 256)
        act[pl.ds(t, count), s] = h.astype(BF16)
        act_up[pl.ds(t, count), s] = moved.astype(BF16)

    whole_groups = (columns // 8) // group

    def first_step(g, carry):
        for s in range(4):
            first_conv(g * group, group, s)
        return carry

    lax.fori_loop(0, whole_groups, first_step, 0)
    for s in range(2):
        first_conv(columns // 8, 1, s)

    zero_part = jnp.zeros((16, 128), F32)

    def second_step(t, carry):
        for half in range(2):
            first_s = 2 * half
            nxt_t, nxt_s = (t, first_s + 2) if half == 0 else (t + 1, 0)
            rows = 2 * PITCH
            top = act[t, first_s : first_s + 2].reshape(rows, 256)
            top_up = act_up[t, first_s : first_s + 2].reshape(rows, 256)
            one = act[t, first_s + 1]
            two = act[nxt_t, nxt_s]
            one_up = act_up[t, first_s + 1]
            two_up = act_up[nxt_t, nxt_s]
            low = jnp.concatenate([one, two], axis=0)
            low_up = jnp.concatenate([one_up, two_up], axis=0)
            left = jnp.concatenate([top, top_up, low, low_up], axis=1)
            h = jnp.dot(left, w2[...], preferred_element_type=F32)
            h = activate(h, bias2, 2, low_2, high_2).astype(BF16)
            for k in range(2):
                parts[t * 4 + first_s + k] = zero_part
                parts[t * 4 + first_s + k, :, 0:PITCH] = lax.dot_general(
                    w3[...], h[k], (((1,), (1,)), ((), ())), preferred_element_type=F32
                )
        return carry

    lax.fori_loop(0, columns // 8, second_step, 0)
    t = columns // 8
    left = jnp.concatenate([act[t, 0], act_up[t, 0], act[t, 1], act_up[t, 1]], axis=1)
    h = jnp.dot(left, w2[...], preferred_element_type=F32)
    h = activate(h, bias2, 1, low_2, high_2).astype(BF16)
    parts[4 * t] = zero_part
    parts[4 * t, :, 0:PITCH] = lax.dot_general(
        w3[...], h[0], (((1,), (1,)), ((), ())), preferred_element_type=F32
    )

    for i in range(columns // 2):
        sums[8 * i : 8 * i + 8, :] = parts[i, 0:8, :] + parts[i + 1, 8:16, :]
    jj = lax.broadcasted_iota(jnp.int32, (128, lat), 0)
    ll = lax.broadcasted_iota(jnp.int32, (128, lat), 1)
    out = jnp.zeros((columns, lat), F32)
    for k in range(4):
        x = sums[pl.ds(k, columns, stride=4), :]
        high = x.astype(BF16)
        rest = (x - high.astype(F32)).astype(BF16)
        put_at = jnp.where(ll == 2 * (jj - k // 2) + k % 2, 1.0, 0.0).astype(BF16)
        out = out + jnp.dot(high, put_at, preferred_element_type=F32)
        out = out + jnp.dot(rest, put_at, preferred_element_type=F32)
    visc_out[...] = jnp.exp(out)


def swap(x, axis, parity, count, periodic):
    pairs = []
    for i in range(count):
        j = i + 1 if i % 2 == parity else i - 1
        if periodic or 0 <= j < count:
            pairs.append((i, j % count))
    return lax.ppermute(x, axis, pairs)


def local(
    nx,
    ny,
    zonal,
    merid,
    thick,
    land,
    visc,
    wind,
    gravity,
    conv_first,
    bias_first,
    conv_second,
    bias_second,
    conv_last,
):
    layers, columns, lat = zonal.shape
    big = pltpu.CompilerParams(vmem_limit_bytes=48 * 1024 * 1024)
    lon_rows = EDGE * FIELDS
    lat_a, lat_b, lon_a, lon_b = pl.pallas_call(
        pack_kernel,
        out_shape=[jax.ShapeDtypeStruct((columns, lat), BF16)] * 2
        + [jax.ShapeDtypeStruct((lon_rows, lat), BF16)] * 2,
        in_specs=[VMEM] * 6,
        out_specs=[VMEM] * 4,
        compiler_params=big,
        name="pack",
    )(zonal, merid, thick, land, visc, wind)
    lat_a = swap(lat_a, "oy", 0, ny, False)
    lat_b = swap(lat_b, "oy", 1, ny, False)
    w1, w2, w3, b1, b2 = pl.pallas_call(
        weight_kernel,
        out_shape=[
            jax.ShapeDtypeStruct((4, 256, 256), BF16),
            jax.ShapeDtypeStruct((1024, 256), BF16),
            jax.ShapeDtypeStruct((16, 256), BF16),
            jax.ShapeDtypeStruct((8, 256), F32),
            jax.ShapeDtypeStruct((8, 256), F32),
        ],
        in_specs=[VMEM] * 5,
        out_specs=[VMEM] * 5,
        compiler_params=big,
        name="weights",
    )(conv_first, conv_second, conv_last, bias_first[None], bias_second[None])
    lon_a, lon_b = pl.pallas_call(
        corner_kernel,
        out_shape=[jax.ShapeDtypeStruct((lon_rows + 32, lat), BF16)] * 2,
        in_specs=[VMEM] * 4,
        out_specs=[VMEM] * 2,
        compiler_params=big,
        name="corners",
    )(lon_a, lon_b, lat_a, lat_b)
    lon_a = swap(lon_a, "ox", 0, nx, True)
    lon_b = swap(lon_b, "ox", 1, nx, True)
    wide = 2 * lat
    outer = columns + 4 * EDGE
    tiles = columns // 8 + 2
    return pl.pallas_call(
        functools.partial(main_kernel, ny),
        out_shape=[jax.ShapeDtypeStruct((layers, columns, lat), F32)] * 3
        + [jax.ShapeDtypeStruct((columns, lat), F32)],
        in_specs=[VMEM] * 6 + [pl.BlockSpec(memory_space=pltpu.SMEM)] + [VMEM] * 9,
        out_specs=[VMEM] * 4,
        scratch_shapes=[
            pltpu.VMEM((FIELDS, outer, wide), F32),
            pltpu.VMEM((layers, outer, wide), F32),
            pltpu.VMEM((layers, outer, wide), F32),
            pltpu.VMEM((columns + 2 * EDGE, 16, wide), F32),
            pltpu.VMEM((tiles, PITCH, 256), BF16),
            pltpu.VMEM((tiles - 1, 4, PITCH, 256), BF16),
            pltpu.VMEM((tiles - 1, 4, PITCH, 256), BF16),
            pltpu.VMEM((columns // 2 + 1, 16, 128), F32),
            pltpu.VMEM((4 * columns, 128), F32),
        ],
        compiler_params=big,
        name="step",
    )(zonal, merid, thick, land, visc, wind, gravity, lat_a, lat_b, lon_a, lon_b, w1, w2, w3, b1, b2)


def solution(mesh):
    in_specs = (
        P(None, "ox", "oy"),
        P(None, "ox", "oy"),
        P(None, "ox", "oy"),
        P("ox", "oy"),
        P("ox", "oy"),
        P(None, "ox", "oy"),
        P(),
        P(),
        P(),
        P(),
        P(),
        P(),
    )
    out_specs = (P(None, "ox", "oy"), P(None, "ox", "oy"), P(None, "ox", "oy"), P("ox", "oy"))
    body = functools.partial(local, mesh.shape["ox"], mesh.shape["oy"])
    return jax.shard_map(body, mesh=mesh, in_specs=in_specs, out_specs=out_specs, check_vma=False)
```

```python
import functools

import jax
import jax.numpy as jnp
from jax import lax
from jax.experimental import pallas as pl
from jax.experimental.pallas import tpu as pltpu
from jax.sharding import PartitionSpec as P

TIME_STEP = 0.05
REST_DEPTH = 1.4
DRAG_RATE = 0.5

F32 = jnp.float32
BF16 = jnp.bfloat16
EDGE = 8
FIELDS = 16
PITCH = 80
VMEM = pl.BlockSpec(memory_space=pltpu.VMEM)


def own_fields(zonal, merid, thick, land, visc, wind, rows):
    sea = land[rows, :].astype(F32)
    layers = zonal.shape[0]
    maps = [zonal[l, rows, :] * sea for l in range(layers)]
    maps += [merid[l, rows, :] * sea for l in range(layers)]
    maps += [thick[l, rows, :] - REST_DEPTH for l in range(layers)]
    return maps + [sea, visc[rows, :], wind[0, rows, :], wind[1, rows, :]]


def pack_kernel(*refs):
    sources, (lat_a, lat_b, lon_a, lon_b), held, sems = refs[:6], refs[6:10], refs[10:16], refs[16:]
    copies = [pltpu.make_async_copy(*each) for each in zip(sources, held, sems)]
    for copy in copies:
        copy.start()
    for copy in copies:
        copy.wait()
    zonal, merid, thick, land, visc, wind = held
    columns, lat = land.shape
    even_y = lax.rem(lax.axis_index("oy"), 2) == 0
    even_x = lax.rem(lax.axis_index("ox"), 2) == 0
    lane = lax.broadcasted_iota(jnp.int32, (16, lat), 1) // EDGE
    maps_low = own_fields(zonal, merid, thick, land, visc, wind, slice(0, EDGE))
    maps_high = own_fields(zonal, merid, thick, land, visc, wind, slice(columns - EDGE, columns))
    for f in range(0, FIELDS, 2):
        low = jnp.concatenate(maps_low[f : f + 2], axis=0)
        high = jnp.concatenate(maps_high[f : f + 2], axis=0)
        lon_a[EDGE * f : EDGE * f + 16, :] = jnp.where(even_x, high, low).astype(BF16)
        lon_b[EDGE * f : EDGE * f + 16, :] = jnp.where(even_x, low, high).astype(BF16)
    for c in range(0, columns, 16):
        low = jnp.zeros((16, lat), F32)
        high = jnp.zeros((16, lat), F32)
        for f, field in enumerate(own_fields(zonal, merid, thick, land, visc, wind, slice(c, c + 16))):
            here = lane == f
            low = jnp.where(here, pltpu.roll(field, EDGE * f % lat, 1), low)
            high = jnp.where(here, pltpu.roll(field, (EDGE * f + EDGE) % lat, 1), high)
        lat_a[c : c + 16, :] = jnp.where(even_y, high, low).astype(BF16)
        lat_b[c : c + 16, :] = jnp.where(even_y, low, high).astype(BF16)


def corner_kernel(lon_a, lon_b, got_a, got_b, out_a, out_b):
    columns = got_a.shape[0]
    even_x = lax.rem(lax.axis_index("ox"), 2) == 0
    size = lon_a.shape[0]
    out_a[0:size, :] = lon_a[...]
    out_b[0:size, :] = lon_b[...]
    for n, got in enumerate((got_a, got_b)):
        low = got[0:16, :]
        high = got[columns - 16 : columns, :]
        out_a[size + 16 * n : size + 16 * n + 16, :] = jnp.where(even_x, high, low)
        out_b[size + 16 * n : size + 16 * n + 16, :] = jnp.where(even_x, low, high)


def weight_kernel(first, second, last, bias_first, bias_second, gravity, w1, w2, w3, b1, b2, grav):
    hidden = second.shape[2]
    zero = jnp.zeros((hidden, hidden), F32)
    turned = [[second[a, b].astype(F32).T * 0.5 for b in range(3)] for a in range(3)]
    tap = lambda a, b: turned[a][b] if 0 <= a < 3 and 0 <= b < 3 else zero
    for px in range(4):
        for py in range(4):
            ex, ey, a, b = px % 2, py % 2, px // 2, py // 2
            row = ((2 * a + b) * 4 + 2 * ex + ey) * hidden
            for dx in range(2):
                w2[row : row + hidden, 128 * dx : 128 * dx + 128] = jnp.concatenate(
                    [tap(px - dx, py), tap(px - dx, py - 1)], axis=1
                ).astype(BF16)
    feats = first.shape[3]
    spot = lax.broadcasted_iota(jnp.int32, (256, feats), 0)
    chan = lax.broadcasted_iota(jnp.int32, (256, feats), 1)
    total = jnp.zeros((256, hidden), F32)
    ddx, ddy = spot // 128, (spot // 64) % 2
    for a in range(3):
        for b in range(3):
            want = ((ddx + a) * 4 + ddy + b) * feats + chan
            place = jnp.where(spot % 64 == want, 0.5, 0.0).astype(BF16)
            total = total + lax.dot_general(
                place, first[a, b], (((1,), (1,)), ((), ())), preferred_element_type=F32
            )
    base = jnp.concatenate(
        [
            jnp.concatenate([total[0:64], total[64:128]], axis=1),
            jnp.concatenate([total[128:192], total[192:256]], axis=1),
        ],
        axis=1,
    )
    for s in range(4):
        off = 80 + 32 * s
        w1[s] = jnp.concatenate(
            [jnp.zeros((off, 256), F32), base, jnp.zeros((192 - off, 256), F32)], axis=0
        ).astype(BF16)
    row = lax.broadcasted_iota(jnp.int32, (16, 128), 0)
    blank = jnp.zeros((1, hidden), F32)
    piece = lambda a, b: last[a, b].astype(F32) if 0 <= a < 3 and 0 <= b < 3 else blank
    for ex in range(2):
        tile = jnp.zeros((16, 128), F32)
        for k in range(16):
            a, dx, b, dy = k // 8, (k // 4) % 2, (k // 2) % 2, k % 2
            p, q = 2 * a + ex - dx, 2 * b - dy
            line = jnp.concatenate([piece(p, q), piece(p, q + 1)], axis=1)
            tile = jnp.where(row == k, jnp.broadcast_to(line, (16, 128)), tile)
        turned_tile = jnp.concatenate([tile] * 8, axis=0).T
        lane = lax.broadcasted_iota(jnp.int32, (128, 128), 1) // 16
        for m in range(8):
            start = 256 * m + 128 * ex
            w3[start : start + 128, :] = jnp.where(lane == m, turned_tile, 0.0).astype(BF16)
    for bias, out in ((bias_first, b1), (bias_second, b2)):
        half = bias[...] * 0.5
        out[...] = jnp.broadcast_to(jnp.concatenate([half] * 4, axis=1), (8, 256))
    for l in range(grav.shape[0]):
        grav[l] = jnp.broadcast_to(gravity[0:1, l : l + 1], grav.shape[1:])


def main_kernel(
    lat_count,
    zonal,
    merid,
    thick,
    land,
    visc,
    wind,
    grav,
    lat_a,
    lat_b,
    lon_a,
    lon_b,
    w1,
    w2,
    w3,
    b1,
    b2,
    zonal_out,
    merid_out,
    thick_out,
    visc_out,
    ext,
    nxt,
    prs,
    spread,
    feat,
    act,
    act_up,
    second,
    parts,
    sums,
):
    layers, columns, lat = zonal.shape
    oy = lax.axis_index("oy")
    even_y = lax.rem(oy, 2) == 0
    even_x = lax.rem(lax.axis_index("ox"), 2) == 0
    base = 2 * EDGE
    wide = 2 * lat
    sea_id, visc_id, wind_id = 3 * layers, 3 * layers + 1, 3 * layers + 2

    west = jnp.where(even_x, lon_b[...], lon_a[...])
    east = jnp.where(even_x, lon_a[...], lon_b[...])
    size = EDGE * FIELDS
    north, south = [], []
    for side, slot in ((west, slice(8, 16)), (east, slice(0, 8))):
        from_a = side[size : size + 16].astype(F32)[slot]
        from_b = side[size + 16 : size + 32].astype(F32)[slot]
        north.append(jnp.where(even_y, from_a, from_b))
        south.append(jnp.where(even_y, from_b, from_a))
    west = west[:size].astype(F32)
    east = east[:size].astype(F32)
    lane = lax.broadcasted_iota(jnp.int32, (EDGE, lat), 1)

    def second_tile(n_rows, s_rows, f):
        up = pltpu.roll(n_rows, (lat - EDGE * f) % lat, 1)
        down = pltpu.roll(s_rows, (2 * lat - EDGE - EDGE * f) % lat, 1)
        return jnp.where(lane < EDGE, up, jnp.where(lane >= lat - EDGE, down, 0.0))

    def put(f, row, first_tile, n_rows, s_rows):
        far = second_tile(n_rows, s_rows, f)
        if 2 * layers <= f < 3 * layers:
            far = far + REST_DEPTH
        ext[f, row : row + EDGE, 0:lat] = first_tile
        ext[f, row : row + EDGE, lat:wide] = far

    for f in range(FIELDS):
        lift = REST_DEPTH if 2 * layers <= f < 3 * layers else 0.0
        put(f, base - EDGE, west[EDGE * f : EDGE * f + EDGE] + lift, north[0], south[0])
        put(f, base + columns, east[EDGE * f : EDGE * f + EDGE] + lift, north[1], south[1])
    for c in range(0, columns, 16):
        got_a = lat_a[c : c + 16, :].astype(F32)
        got_b = lat_b[c : c + 16, :].astype(F32)
        n_both = jnp.where(even_y, got_a, got_b)
        s_both = jnp.where(even_y, got_b, got_a)
        for h in range(0, 16, EDGE):
            rows = slice(c + h, c + h + EDGE)
            sea = land[rows, :].astype(F32)
            maps = [zonal[l, rows, :] * sea for l in range(layers)]
            maps += [merid[l, rows, :] * sea for l in range(layers)]
            maps += [thick[l, rows, :] for l in range(layers)]
            maps += [sea, visc[rows, :], wind[0, rows, :], wind[1, rows, :]]
            for f in range(FIELDS):
                put(f, base + c + h, maps[f], n_both[h : h + EDGE], s_both[h : h + EDGE])

    def up(x):
        return pltpu.roll(x, wide - 1, 1)

    def down(x):
        return pltpu.roll(x, 1, 1)

    chunks = (columns + 2 * EDGE) // EDGE
    for ch in range(chunks):
        r = EDGE + EDGE * ch
        here, plus, minus = slice(r, r + 8), slice(r + 1, r + 9), slice(r - 1, r + 7)
        sea = ext[sea_id, here, :]
        odd = []
        for l in range(layers):
            h = ext[2 * layers + l, here, :]
            flux_e = ext[l, plus, :] * ext[2 * layers + l, plus, :]
            flux_w = ext[l, minus, :] * ext[2 * layers + l, minus, :]
            flux_y = ext[layers + l, here, :] * h
            diverge = (flux_e - flux_w) * 0.5 + (up(flux_y) - down(flux_y)) * 0.5
            h = h - TIME_STEP * sea * diverge
            nxt[l, r : r + 8, :] = h
            if 1 <= ch < chunks - 1:
                thick_out[l, r - base : r - base + 8, :] = h[:, 0:lat]
            odd.append(h - REST_DEPTH)
        for l in reversed(range(layers - 1)):
            odd[l] = odd[l] + odd[l + 1]
        total = jnp.zeros_like(sea)
        for l in range(layers):
            total = total + grav[l] * odd[l]
            prs[l, r : r + 8, :] = total

    place = lax.broadcasted_iota(jnp.int32, (EDGE, wide), 1)
    place = jnp.where(place < lat + lat // 2, place, place - wide)
    total_rows = lat_count * lat
    coriolis = 0.3 + 1.4 * ((oy * lat + place).astype(F32) + 0.5) / total_rows
    in_lat = (place >= -3) & (place < lat + 3)
    for ch in range(chunks):
        r = EDGE + EDGE * ch
        here, plus, minus = slice(r, r + 8), slice(r + 1, r + 9), slice(r - 1, r + 7)
        sea = ext[sea_id, here, :]
        v = ext[visc_id, here, :]
        mix = [
            0.5 * (v + ext[visc_id, plus, :]),
            0.5 * (v + ext[visc_id, minus, :]),
            0.5 * (v + up(v)),
            0.5 * (v + down(v)),
        ]

        def lap(f, q):
            near = (ext[f, plus, :], ext[f, minus, :], up(q), down(q))
            total = mix[0] * (near[0] - q)
            for side in range(1, 4):
                total = total + mix[side] * (near[side] - q)
            return total

        heavy = jnp.zeros_like(sea)
        moving = jnp.zeros_like(sea)
        for l in range(layers):
            zm = ext[l, here, :]
            vm = ext[layers + l, here, :]
            p = prs[l, here, :]
            h = nxt[l, here, :]
            grad_x = (prs[l, plus, :] - prs[l, minus, :]) * 0.5
            grad_y = (up(p) - down(p)) * 0.5
            push_x = coriolis * vm - grad_x + lap(l, zm)
            push_y = -coriolis * zm - grad_y + lap(layers + l, vm)
            if l == 0:
                push_x = push_x + ext[wind_id, here, :] / h
                push_y = push_y + ext[wind_id + 1, here, :] / h
            if l == layers - 1:
                push_x = push_x - DRAG_RATE * zm
                push_y = push_y - DRAG_RATE * vm
            zn = sea * (zm + TIME_STEP * push_x)
            vn = sea * (vm + TIME_STEP * push_y)
            if 1 <= ch < chunks - 1:
                zonal_out[l, r - base : r - base + 8, :] = zn[:, 0:lat]
                merid_out[l, r - base : r - base + 8, :] = vn[:, 0:lat]
            heavy = heavy + h
            moving = moving + h * (zn * zn + vn * vn)
            if l == 0:
                maps = [zn, vn, sea * (h - REST_DEPTH)]
        maps.append(sea * (0.5 * moving / heavy))
        keep = in_lat
        if ch == 0 or ch == chunks - 1:
            column = lax.broadcasted_iota(jnp.int32, (EDGE, wide), 0) + (r - base)
            keep = keep & (column >= -3) & (column < columns + 3)
        for f, m in enumerate(maps):
            m = jnp.where(keep, m, 0.0)
            for dy in range(4):
                spread[EDGE * ch : EDGE * ch + 8, 4 * dy + f, :] = pltpu.roll(m, (wide - dy) % wide, 1) if dy else m

    block = lax.broadcasted_iota(jnp.int32, (PITCH, wide), 0)
    source = lax.broadcasted_iota(jnp.int32, (PITCH, wide), 1)
    blocks = lat // 2 + 2
    chooser = jnp.where(
        (block < blocks) & (source == lax.rem(wide - 3 + 2 * block, wide)), 1.0, 0.0
    ).astype(BF16)
    tiles = (columns + 2 * EDGE) // 8
    for t in range(0, tiles, 2):
        got = spread[8 * t : 8 * t + 16].reshape(256, wide).astype(BF16)
        g = lax.dot_general(
            chooser, got, (((1,), (1,)), ((), ())), preferred_element_type=F32
        ).astype(BF16)
        feat[t] = g
        if t + 1 < tiles - 1:
            feat[t + 1, :, 0:128] = g[:, 128:256]
        if t > 0:
            feat[t - 1, :, 128:256] = g[:, 0:128]

    south_end = jnp.where(oy == 0, 0.0, 1.0)
    north_end = jnp.where(oy == lat_count - 1, 0.0, 1.0)
    brow = lax.broadcasted_iota(jnp.int32, (8, 256), 0)
    quad = lax.broadcasted_iota(jnp.int32, (8, 256), 1) // 64 % 2
    low_1 = jnp.where(brow == 0, south_end, 1.0)
    high_1 = jnp.where(brow == blocks - 1 - 64, north_end, 1.0)
    low_2 = jnp.where((brow == 0) & (quad == 0), south_end, 1.0)
    high_2 = jnp.where((brow == blocks - 2 - 64) & (quad == 1), north_end, 1.0)

    def activate(total, bias, count, low, high):
        total = total + bias
        total = total * jnp.tanh(total) + total
        total = total.reshape(count, PITCH, 256)
        return jnp.concatenate(
            [total[:, 0:8] * low, total[:, 8:64], total[:, 64:72] * high, total[:, 72:]], axis=1
        )

    bias1 = b1[0:1, :]
    bias2 = b2[0:1, :]
    groups = feat.shape[0]

    def first_step(n, carry):
        left = feat[...].reshape(groups * PITCH, 256)
        h = jnp.dot(left, w1[n], preferred_element_type=F32)
        h = activate(h, bias1, groups, low_1, high_1)
        moved = pltpu.roll(h.reshape(groups * PITCH, 256), groups * PITCH - 1, 0)
        act[:, n] = h.astype(BF16)
        act_up[:, n] = moved.reshape(groups, PITCH, 256).astype(BF16)
        return carry

    lax.fori_loop(0, 4, first_step, 0)

    block_rows = columns // 2 + 1
    some = next(n for n in range(16, 0, -1) if block_rows % n == 0)
    flat = lambda ref: ref.reshape(4 * groups, PITCH, 256)
    first_act, first_up = flat(act), flat(act_up)

    def second_step(n, carry):
        at = n * some
        parts_of = [
            ref[pl.ds(at + shift, some)].reshape(some * PITCH, 256)
            for shift in range(2)
            for ref in (first_act, first_up)
        ]
        h = jnp.dot(jnp.concatenate(parts_of, axis=1), w2[...], preferred_element_type=F32)
        second[pl.ds(at, some)] = activate(h, bias2, some, low_2, high_2).astype(BF16)
        return carry

    lax.fori_loop(0, block_rows // some, second_step, 0)

    eights = columns // 16
    wide_left = [
        jnp.concatenate([second[8 * g + m] for g in range(eights)], axis=0) for m in range(8)
    ]
    last = jnp.dot(jnp.concatenate(wide_left, axis=1), w3[...], preferred_element_type=F32)
    pad = jnp.zeros((128 - PITCH, 128), F32)
    for g in range(eights):
        parts[128 * g : 128 * g + 128, :] = jnp.concatenate([last[PITCH * g : PITCH * (g + 1)], pad], axis=0).T
    end = jnp.dot(second[8 * eights], w3[0:256], preferred_element_type=F32)
    parts[128 * eights : 128 * eights + 16, :] = jnp.concatenate([end, pad], axis=0).T[0:16]

    for i in range(columns // 2):
        sums[8 * i : 8 * i + 8, :] = parts[16 * i : 16 * i + 8, :] + parts[16 * i + 24 : 16 * i + 32, :]
    jj = lax.broadcasted_iota(jnp.int32, (128, lat), 0)
    ll = lax.broadcasted_iota(jnp.int32, (128, lat), 1)
    out = jnp.zeros((columns, lat), F32)
    for k in range(4):
        x = sums[pl.ds(k, columns, stride=4), :]
        high = x.astype(BF16)
        rest = (x - high.astype(F32)).astype(BF16)
        put_at = jnp.where(ll == 2 * (jj - k // 2) + k % 2, 1.0, 0.0).astype(BF16)
        out = out + jnp.dot(high, put_at, preferred_element_type=F32)
        out = out + jnp.dot(rest, put_at, preferred_element_type=F32)
    visc_out[...] = jnp.exp(out)


def swap(x, axis, parity, count, periodic):
    pairs = []
    for i in range(count):
        j = i + 1 if i % 2 == parity else i - 1
        if periodic or 0 <= j < count:
            pairs.append((i, j % count))
    return lax.ppermute(x, axis, pairs)


def local(
    nx,
    ny,
    zonal,
    merid,
    thick,
    land,
    visc,
    wind,
    gravity,
    conv_first,
    bias_first,
    conv_second,
    bias_second,
    conv_last,
):
    layers, columns, lat = zonal.shape
    big = pltpu.CompilerParams(vmem_limit_bytes=48 * 1024 * 1024)
    lon_rows = EDGE * FIELDS
    lat_a, lat_b, lon_a, lon_b = pl.pallas_call(
        pack_kernel,
        out_shape=[jax.ShapeDtypeStruct((columns, lat), BF16)] * 2
        + [jax.ShapeDtypeStruct((lon_rows, lat), BF16)] * 2,
        in_specs=[pl.BlockSpec(memory_space=pltpu.HBM)] * 6,
        out_specs=[VMEM] * 4,
        scratch_shapes=[pltpu.VMEM(a.shape, a.dtype) for a in (zonal, merid, thick, land, visc, wind)]
        + [pltpu.SemaphoreType.DMA] * 6,
        compiler_params=big,
        name="pack",
    )(zonal, merid, thick, land, visc, wind)
    lat_a = swap(lat_a, "oy", 0, ny, False)
    lat_b = swap(lat_b, "oy", 1, ny, False)
    w1, w2, w3, b1, b2, grav = pl.pallas_call(
        weight_kernel,
        out_shape=[
            jax.ShapeDtypeStruct((4, 256, 256), BF16),
            jax.ShapeDtypeStruct((1024, 256), BF16),
            jax.ShapeDtypeStruct((2048, 128), BF16),
            jax.ShapeDtypeStruct((8, 256), F32),
            jax.ShapeDtypeStruct((8, 256), F32),
            jax.ShapeDtypeStruct((layers, 8, 2 * lat), F32),
        ],
        in_specs=[VMEM] * 6,
        out_specs=[VMEM] * 6,
        compiler_params=big,
        name="weights",
    )(conv_first, conv_second, conv_last, bias_first[None], bias_second[None], gravity[None])
    lon_a, lon_b = pl.pallas_call(
        corner_kernel,
        out_shape=[jax.ShapeDtypeStruct((lon_rows + 32, lat), BF16)] * 2,
        in_specs=[VMEM] * 4,
        out_specs=[VMEM] * 2,
        compiler_params=big,
        name="corners",
    )(lon_a, lon_b, lat_a, lat_b)
    lon_a = swap(lon_a, "ox", 0, nx, True)
    lon_b = swap(lon_b, "ox", 1, nx, True)
    wide = 2 * lat
    outer = columns + 4 * EDGE
    tiles = columns // 8 + 2
    return pl.pallas_call(
        functools.partial(main_kernel, ny),
        out_shape=[jax.ShapeDtypeStruct((layers, columns, lat), F32)] * 3
        + [jax.ShapeDtypeStruct((columns, lat), F32)],
        in_specs=[VMEM] * 16,
        out_specs=[VMEM] * 4,
        scratch_shapes=[
            pltpu.VMEM((FIELDS, outer, wide), F32),
            pltpu.VMEM((layers, outer, wide), F32),
            pltpu.VMEM((layers, outer, wide), F32),
            pltpu.VMEM((columns + 2 * EDGE, 16, wide), F32),
            pltpu.VMEM((tiles - 1, PITCH, 256), BF16),
            pltpu.VMEM((tiles - 1, 4, PITCH, 256), BF16),
            pltpu.VMEM((tiles - 1, 4, PITCH, 256), BF16),
            pltpu.VMEM((columns // 2 + 1, PITCH, 256), BF16),
            pltpu.VMEM((8 * columns + 16, 128), F32),
            pltpu.VMEM((4 * columns, 128), F32),
        ],
        compiler_params=big,
        name="step",
    )(zonal, merid, thick, land, visc, wind, grav, lat_a, lat_b, lon_a, lon_b, w1, w2, w3, b1, b2)


def solution(mesh):
    in_specs = (
        P(None, "ox", "oy"),
        P(None, "ox", "oy"),
        P(None, "ox", "oy"),
        P("ox", "oy"),
        P("ox", "oy"),
        P(None, "ox", "oy"),
        P(),
        P(),
        P(),
        P(),
        P(),
        P(),
    )
    out_specs = (P(None, "ox", "oy"), P(None, "ox", "oy"), P(None, "ox", "oy"), P("ox", "oy"))
    body = functools.partial(local, mesh.shape["ox"], mesh.shape["oy"])
    return jax.shard_map(body, mesh=mesh, in_specs=in_specs, out_specs=out_specs, check_vma=False)
```

```python
import functools

import jax
import jax.numpy as jnp
from jax import lax
from jax.experimental import pallas as pl
from jax.experimental.pallas import tpu as pltpu
from jax.sharding import PartitionSpec as P

TIME_STEP = 0.05
REST_DEPTH = 1.4
DRAG_RATE = 0.5

F32 = jnp.float32
BF16 = jnp.bfloat16
EDGE = 8
FIELDS = 16
PITCH = 80
VMEM = pl.BlockSpec(memory_space=pltpu.VMEM)


def own_fields(zonal, merid, thick, land, visc, wind, rows):
    sea = land[rows, :].astype(F32)
    layers = zonal.shape[0]
    maps = [zonal[l, rows, :] * sea for l in range(layers)]
    maps += [merid[l, rows, :] * sea for l in range(layers)]
    maps += [thick[l, rows, :] - REST_DEPTH for l in range(layers)]
    return maps + [sea, visc[rows, :], wind[0, rows, :], wind[1, rows, :]]


def pack_kernel(*refs):
    sources, (lat_a, lat_b), held, sems = refs[:6], refs[6:8], refs[8:14], refs[14:]
    copies = [pltpu.make_async_copy(*each) for each in zip(sources, held, sems)]
    for copy in copies:
        copy.start()
    for copy in copies:
        copy.wait()
    zonal, merid, thick, land, visc, wind = held
    columns, lat = land.shape
    even_y = lax.rem(lax.axis_index("oy"), 2) == 0
    lane = lax.broadcasted_iota(jnp.int32, (16, lat), 1) // EDGE
    for c in range(0, columns, 16):
        low = jnp.zeros((16, lat), F32)
        high = jnp.zeros((16, lat), F32)
        for f, field in enumerate(own_fields(zonal, merid, thick, land, visc, wind, slice(c, c + 16))):
            here = lane == f
            low = jnp.where(here, pltpu.roll(field, EDGE * f % lat, 1), low)
            high = jnp.where(here, pltpu.roll(field, (EDGE * f + EDGE) % lat, 1), high)
        lat_a[c : c + 16, :] = jnp.where(even_y, high, low).astype(BF16)
        lat_b[c : c + 16, :] = jnp.where(even_y, low, high).astype(BF16)


def lon_kernel(zonal, merid, thick, land, visc, wind, got_a, got_b, after, lon_a, lon_b):
    del after
    columns = got_a.shape[0]
    even_x = lax.rem(lax.axis_index("ox"), 2) == 0
    size = EDGE * FIELDS
    maps_low = own_fields(zonal, merid, thick, land, visc, wind, slice(0, EDGE))
    maps_high = own_fields(zonal, merid, thick, land, visc, wind, slice(columns - EDGE, columns))
    for f in range(0, FIELDS, 2):
        low = jnp.concatenate(maps_low[f : f + 2], axis=0)
        high = jnp.concatenate(maps_high[f : f + 2], axis=0)
        lon_a[EDGE * f : EDGE * f + 16, :] = jnp.where(even_x, high, low).astype(BF16)
        lon_b[EDGE * f : EDGE * f + 16, :] = jnp.where(even_x, low, high).astype(BF16)
    for n, got in enumerate((got_a, got_b)):
        low = got[0:16, :]
        high = got[columns - 16 : columns, :]
        lon_a[size + 16 * n : size + 16 * n + 16, :] = jnp.where(even_x, high, low)
        lon_b[size + 16 * n : size + 16 * n + 16, :] = jnp.where(even_x, low, high)


def weight_kernel(first, second, last, bias_first, bias_second, gravity, w1, w2, w3, b1, b2, grav):
    hidden = second.shape[2]
    zero = jnp.zeros((hidden, hidden), F32)
    turned = [[second[a, b].astype(F32).T * 0.5 for b in range(3)] for a in range(3)]
    tap = lambda a, b: turned[a][b] if 0 <= a < 3 and 0 <= b < 3 else zero
    for px in range(4):
        for py in range(4):
            ex, ey, a, b = px % 2, py % 2, px // 2, py // 2
            row = ((2 * a + b) * 4 + 2 * ex + ey) * hidden
            for dx in range(2):
                w2[row : row + hidden, 128 * dx : 128 * dx + 128] = jnp.concatenate(
                    [tap(px - dx, py), tap(px - dx, py - 1)], axis=1
                ).astype(BF16)
    feats = first.shape[3]
    spot = lax.broadcasted_iota(jnp.int32, (256, feats), 0)
    chan = lax.broadcasted_iota(jnp.int32, (256, feats), 1)
    total = jnp.zeros((256, hidden), F32)
    ddx, ddy = spot // 128, (spot // 64) % 2
    for a in range(3):
        for b in range(3):
            want = ((ddx + a) * 4 + ddy + b) * feats + chan
            place = jnp.where(spot % 64 == want, 0.5, 0.0).astype(BF16)
            total = total + lax.dot_general(
                place, first[a, b], (((1,), (1,)), ((), ())), preferred_element_type=F32
            )
    base = jnp.concatenate(
        [
            jnp.concatenate([total[0:64], total[64:128]], axis=1),
            jnp.concatenate([total[128:192], total[192:256]], axis=1),
        ],
        axis=1,
    )
    for s in range(4):
        off = 80 + 32 * s
        w1[s] = jnp.concatenate(
            [jnp.zeros((off, 256), F32), base, jnp.zeros((192 - off, 256), F32)], axis=0
        ).astype(BF16)
    row = lax.broadcasted_iota(jnp.int32, (16, 128), 0)
    blank = jnp.zeros((1, hidden), F32)
    piece = lambda a, b: last[a, b].astype(F32) if 0 <= a < 3 and 0 <= b < 3 else blank
    for ex in range(2):
        tile = jnp.zeros((16, 128), F32)
        for k in range(16):
            a, dx, b, dy = k // 8, (k // 4) % 2, (k // 2) % 2, k % 2
            p, q = 2 * a + ex - dx, 2 * b - dy
            line = jnp.concatenate([piece(p, q), piece(p, q + 1)], axis=1)
            tile = jnp.where(row == k, jnp.broadcast_to(line, (16, 128)), tile)
        turned_tile = jnp.concatenate([tile] * 8, axis=0).T
        lane = lax.broadcasted_iota(jnp.int32, (128, 128), 1) // 16
        for m in range(8):
            start = 256 * m + 128 * ex
            w3[start : start + 128, :] = jnp.where(lane == m, turned_tile, 0.0).astype(BF16)
    for bias, out in ((bias_first, b1), (bias_second, b2)):
        half = bias[...] * 0.5
        out[...] = jnp.broadcast_to(jnp.concatenate([half] * 4, axis=1), (8, 256))
    for l in range(grav.shape[0]):
        grav[l] = jnp.broadcast_to(gravity[0:1, l : l + 1], grav.shape[1:])


def far_tile(n_rows, s_rows, f):
    lat = n_rows.shape[1]
    lane = lax.broadcasted_iota(jnp.int32, n_rows.shape, 1)
    up = pltpu.roll(n_rows, (lat - EDGE * f) % lat, 1)
    down = pltpu.roll(s_rows, (2 * lat - EDGE - EDGE * f) % lat, 1)
    return jnp.where(lane < EDGE, up, jnp.where(lane >= lat - EDGE, down, 0.0))


def dynamics(layers, columns, lat, lat_count, ext, nxt, prs, spread, grav, store):
    oy = lax.axis_index("oy")
    base = 2 * EDGE
    wide = 2 * lat
    chunks = (columns + 2 * EDGE) // EDGE
    sea_id, visc_id, wind_id = 3 * layers, 3 * layers + 1, 3 * layers + 2
    place = lax.broadcasted_iota(jnp.int32, (EDGE, wide), 1)
    place = jnp.where(place < lat + lat // 2, place, place - wide)
    coriolis = 0.3 + 1.4 * ((oy * lat + place).astype(F32) + 0.5) / (lat_count * lat)
    in_lat = (place >= -3) & (place < lat + 3)

    def up(x):
        return pltpu.roll(x, wide - 1, 1)

    def down(x):
        return pltpu.roll(x, 1, 1)

    def rows_of(ch):
        r = EDGE + EDGE * ch
        return slice(r, r + 8), slice(r + 1, r + 9), slice(r - 1, r + 7)

    def thickness(ch):
        here, plus, minus = rows_of(ch)
        sea = ext[sea_id, here, :]
        odd = []
        for l in range(layers):
            h = ext[2 * layers + l, here, :]
            flux_e = ext[l, plus, :] * ext[2 * layers + l, plus, :]
            flux_w = ext[l, minus, :] * ext[2 * layers + l, minus, :]
            flux_y = ext[layers + l, here, :] * h
            diverge = (flux_e - flux_w) * 0.5 + (up(flux_y) - down(flux_y)) * 0.5
            h = h - TIME_STEP * sea * diverge
            nxt[l, here, :] = h
            odd.append(h - REST_DEPTH)
        for l in reversed(range(layers - 1)):
            odd[l] = odd[l] + odd[l + 1]
        total = jnp.zeros_like(sea)
        for l in range(layers):
            total = total + grav[l] * odd[l]
            prs[l, here, :] = total

    def velocity(ch):
        here, plus, minus = rows_of(ch)
        sea = ext[sea_id, here, :]
        v = ext[visc_id, here, :]
        mix = [
            0.5 * (v + ext[visc_id, plus, :]),
            0.5 * (v + ext[visc_id, minus, :]),
            0.5 * (v + up(v)),
            0.5 * (v + down(v)),
        ]

        def lap(f, q):
            near = (ext[f, plus, :], ext[f, minus, :], up(q), down(q))
            total = mix[0] * (near[0] - q)
            for side in range(1, 4):
                total = total + mix[side] * (near[side] - q)
            return total

        heavy = jnp.zeros_like(sea)
        moving = jnp.zeros_like(sea)
        for l in range(layers):
            zm = ext[l, here, :]
            vm = ext[layers + l, here, :]
            p = prs[l, here, :]
            h = nxt[l, here, :]
            grad_x = (prs[l, plus, :] - prs[l, minus, :]) * 0.5
            grad_y = (up(p) - down(p)) * 0.5
            push_x = coriolis * vm - grad_x + lap(l, zm)
            push_y = -coriolis * zm - grad_y + lap(layers + l, vm)
            if l == 0:
                push_x = push_x + ext[wind_id, here, :] / h
                push_y = push_y + ext[wind_id + 1, here, :] / h
            if l == layers - 1:
                push_x = push_x - DRAG_RATE * zm
                push_y = push_y - DRAG_RATE * vm
            zn = sea * (zm + TIME_STEP * push_x)
            vn = sea * (vm + TIME_STEP * push_y)
            store(ch, l, zn[:, 0:lat], vn[:, 0:lat], h[:, 0:lat])
            heavy = heavy + h
            moving = moving + h * (zn * zn + vn * vn)
            if l == 0:
                maps = [zn, vn, sea * (h - REST_DEPTH)]
        maps.append(sea * (0.5 * moving / heavy))
        keep = in_lat
        if ch == 0 or ch == chunks - 1:
            column = lax.broadcasted_iota(jnp.int32, (EDGE, wide), 0) + (EDGE + EDGE * ch - base)
            keep = keep & (column >= -3) & (column < columns + 3)
        for f, m in enumerate(maps):
            m = jnp.where(keep, m, 0.0)
            for dy in range(4):
                spread[EDGE * ch : EDGE * ch + 8, 4 * dy + f, :] = pltpu.roll(m, (wide - dy) % wide, 1) if dy else m

    return thickness, velocity


def block_features(spread, lat):
    wide = 2 * lat
    block = lax.broadcasted_iota(jnp.int32, (PITCH, wide), 0)
    source = lax.broadcasted_iota(jnp.int32, (PITCH, wide), 1)
    chooser = jnp.where(
        (block < lat // 2 + 2) & (source == lax.rem(wide - 3 + 2 * block, wide)), 1.0, 0.0
    ).astype(BF16)

    def take(t):
        got = spread[8 * t : 8 * t + 16].reshape(256, wide).astype(BF16)
        return lax.dot_general(
            chooser, got, (((1,), (1,)), ((), ())), preferred_element_type=F32
        ).astype(BF16)

    return take


def inner_kernel(
    lat_count,
    zonal,
    merid,
    thick,
    land,
    visc,
    wind,
    grav,
    lat_a,
    lat_b,
    zonal_out,
    merid_out,
    thick_out,
    feat,
    edge_ext,
    edge_prs,
    ext,
    nxt,
    prs,
    spread,
):
    layers, columns, lat = zonal.shape
    even_y = lax.rem(lax.axis_index("oy"), 2) == 0
    base = 2 * EDGE
    wide = 2 * lat
    for c in range(0, columns, 16):
        got_a = lat_a[c : c + 16, :].astype(F32)
        got_b = lat_b[c : c + 16, :].astype(F32)
        n_both = jnp.where(even_y, got_a, got_b)
        s_both = jnp.where(even_y, got_b, got_a)
        for h in range(0, 16, EDGE):
            rows = slice(c + h, c + h + EDGE)
            sea = land[rows, :].astype(F32)
            maps = [zonal[l, rows, :] * sea for l in range(layers)]
            maps += [merid[l, rows, :] * sea for l in range(layers)]
            maps += [thick[l, rows, :] for l in range(layers)]
            maps += [sea, visc[rows, :], wind[0, rows, :], wind[1, rows, :]]
            for f in range(FIELDS):
                far = far_tile(n_both[h : h + EDGE], s_both[h : h + EDGE], f)
                if 2 * layers <= f < 3 * layers:
                    far = far + REST_DEPTH
                row = base + c + h
                ext[f, row : row + EDGE, 0:lat] = maps[f]
                ext[f, row : row + EDGE, lat:wide] = far
                edge = {0: 0, EDGE: EDGE, columns - 16: 16, columns - EDGE: 24}.get(c + h)
                if edge is not None:
                    edge_ext[f, edge : edge + EDGE, 0:lat] = maps[f]
                    edge_ext[f, edge : edge + EDGE, lat:wide] = far

    def store(ch, l, zn, vn, h):
        row = EDGE * ch - EDGE
        zonal_out[l, row : row + 8, :] = zn
        merid_out[l, row : row + 8, :] = vn
        thick_out[l, row : row + 8, :] = h

    thickness, velocity = dynamics(layers, columns, lat, lat_count, ext, nxt, prs, spread, grav, store)
    own = columns // EDGE
    for ch in range(1, own + 1):
        thickness(ch)
    for l in range(layers):
        edge_prs[l, 0:8, :] = prs[l, base + EDGE : base + 2 * EDGE, :]
        edge_prs[l, 8:16, :] = prs[l, base + columns - 2 * EDGE : base + columns - EDGE, :]
    for ch in range(2, own):
        velocity(ch)
    take = block_features(spread, lat)
    for t in range(2, own, 2):
        g = take(t)
        feat[t] = g
        feat[t + 1, :, 0:128] = g[:, 128:256]
        feat[t - 1, :, 128:256] = g[:, 0:128]


def main_kernel(
    lat_count,
    zonal_in,
    merid_in,
    thick_in,
    grav,
    lon_a,
    lon_b,
    inner_feat,
    edge_ext,
    edge_prs,
    w1,
    w2,
    w3,
    b1,
    b2,
    zonal_out,
    merid_out,
    thick_out,
    visc_out,
    ext,
    nxt,
    prs,
    spread,
    feat,
    act,
    act_up,
    second,
    parts,
    sums,
    edge_out,
    sems,
):
    columns, lat = visc_out.shape
    layers = grav.shape[0]
    oy = lax.axis_index("oy")
    even_y = lax.rem(oy, 2) == 0
    even_x = lax.rem(lax.axis_index("ox"), 2) == 0
    base = 2 * EDGE
    wide = 2 * lat
    own = columns // EDGE

    west = jnp.where(even_x, lon_b[...], lon_a[...])
    east = jnp.where(even_x, lon_a[...], lon_b[...])
    size = EDGE * FIELDS
    for side, slot, row in ((west, slice(8, 16), base - EDGE), (east, slice(0, 8), base + columns)):
        from_a = side[size : size + 16].astype(F32)[slot]
        from_b = side[size + 16 : size + 32].astype(F32)[slot]
        north = jnp.where(even_y, from_a, from_b)
        south = jnp.where(even_y, from_b, from_a)
        near = side[:size].astype(F32)
        for f in range(FIELDS):
            lift = REST_DEPTH if 2 * layers <= f < 3 * layers else 0.0
            ext[f, row : row + EDGE, 0:lat] = near[EDGE * f : EDGE * f + EDGE] + lift
            ext[f, row : row + EDGE, lat:wide] = far_tile(north, south, f) + lift
    for f in range(FIELDS):
        ext[f, base : base + 16, :] = edge_ext[f, 0:16, :]
        ext[f, base + columns - 16 : base + columns, :] = edge_ext[f, 16:32, :]
    for l in range(layers):
        prs[l, base + EDGE : base + 2 * EDGE, :] = edge_prs[l, 0:8, :]
        prs[l, base + columns - 2 * EDGE : base + columns - EDGE, :] = edge_prs[l, 8:16, :]

    def store(ch, l, zn, vn, h):
        if ch in (1, own):
            side = 0 if ch == 1 else 1
            for k, tile in enumerate((zn, vn, h)):
                edge_out[k, side, l] = tile

    thickness, velocity = dynamics(layers, columns, lat, lat_count, ext, nxt, prs, spread, grav, store)
    edges = (0, 1, own, own + 1)
    for ch in edges:
        thickness(ch)

    for ch in edges:
        velocity(ch)
    copies = [
        pltpu.make_async_copy(
            edge_out.at[k, side],
            out.at[:, pl.ds(side * (columns - EDGE), EDGE), :],
            sems.at[k, side],
        )
        for k, out in enumerate((zonal_out, merid_out, thick_out))
        for side in range(2)
    ]
    for copy in copies:
        copy.start()

    take = block_features(spread, lat)
    blocks = lat // 2 + 2
    first, last = take(0), take(own)
    feat[0] = first
    feat[1, :, 0:128] = first[:, 128:256]
    feat[1, :, 128:256] = inner_feat[1, :, 128:256]
    feat[2, :, 0:128] = inner_feat[own - 1, :, 0:128]
    feat[2, :, 128:256] = last[:, 0:128]
    feat[3] = last

    south_end = jnp.where(oy == 0, 0.0, 1.0)
    north_end = jnp.where(oy == lat_count - 1, 0.0, 1.0)
    brow = lax.broadcasted_iota(jnp.int32, (8, 256), 0)
    quad = lax.broadcasted_iota(jnp.int32, (8, 256), 1) // 64 % 2
    low_1 = jnp.where(brow == 0, south_end, 1.0)
    high_1 = jnp.where(brow == blocks - 1 - 64, north_end, 1.0)
    low_2 = jnp.where((brow == 0) & (quad == 0), south_end, 1.0)
    high_2 = jnp.where((brow == blocks - 2 - 64) & (quad == 1), north_end, 1.0)

    def activate(total, bias, count, low, high):
        total = total + bias
        total = total * jnp.tanh(total) + total
        total = total.reshape(count, PITCH, 256)
        return jnp.concatenate(
            [total[:, 0:8] * low, total[:, 8:64], total[:, 64:72] * high, total[:, 72:]], axis=1
        )

    bias1 = b1[0:1, :]
    bias2 = b2[0:1, :]
    groups = inner_feat.shape[0]

    def first_step(n, carry):
        left = jnp.concatenate([feat[0:2], inner_feat[2 : own - 1], feat[2:4]], axis=0).reshape(groups * PITCH, 256)
        h = jnp.dot(left, w1[n], preferred_element_type=F32)
        h = activate(h, bias1, groups, low_1, high_1)
        moved = pltpu.roll(h.reshape(groups * PITCH, 256), groups * PITCH - 1, 0)
        act[:, n] = h.astype(BF16)
        act_up[:, n] = moved.reshape(groups, PITCH, 256).astype(BF16)
        return carry

    lax.fori_loop(0, 4, first_step, 0)

    block_rows = columns // 2 + 1
    some = next(n for n in range(16, 0, -1) if block_rows % n == 0)
    flat = lambda ref: ref.reshape(4 * groups, PITCH, 256)
    first_act, first_up = flat(act), flat(act_up)

    def second_step(n, carry):
        at = n * some
        parts_of = [
            ref[pl.ds(at + shift, some)].reshape(some * PITCH, 256)
            for shift in range(2)
            for ref in (first_act, first_up)
        ]
        h = jnp.dot(jnp.concatenate(parts_of, axis=1), w2[...], preferred_element_type=F32)
        second[pl.ds(at, some)] = activate(h, bias2, some, low_2, high_2).astype(BF16)
        return carry

    lax.fori_loop(0, block_rows // some, second_step, 0)

    eights = columns // 16
    wide_left = [
        jnp.concatenate([second[8 * g + m] for g in range(eights)], axis=0) for m in range(8)
    ]
    total = jnp.dot(jnp.concatenate(wide_left, axis=1), w3[...], preferred_element_type=F32)
    pad = jnp.zeros((128 - PITCH, 128), F32)
    for g in range(eights):
        parts[128 * g : 128 * g + 128, :] = jnp.concatenate([total[PITCH * g : PITCH * (g + 1)], pad], axis=0).T
    end = jnp.dot(second[8 * eights], w3[0:256], preferred_element_type=F32)
    parts[128 * eights : 128 * eights + 16, :] = jnp.concatenate([end, pad], axis=0).T[0:16]

    for i in range(columns // 2):
        sums[8 * i : 8 * i + 8, :] = parts[16 * i : 16 * i + 8, :] + parts[16 * i + 24 : 16 * i + 32, :]
    jj = lax.broadcasted_iota(jnp.int32, (128, lat), 0)
    ll = lax.broadcasted_iota(jnp.int32, (128, lat), 1)
    out = jnp.zeros((columns, lat), F32)
    for k in range(4):
        x = sums[pl.ds(k, columns, stride=4), :]
        high = x.astype(BF16)
        rest = (x - high.astype(F32)).astype(BF16)
        put_at = jnp.where(ll == 2 * (jj - k // 2) + k % 2, 1.0, 0.0).astype(BF16)
        out = out + jnp.dot(high, put_at, preferred_element_type=F32)
        out = out + jnp.dot(rest, put_at, preferred_element_type=F32)
    visc_out[...] = jnp.exp(out)
    for copy in copies:
        copy.wait()


def swap(x, axis, parity, count, periodic):
    pairs = []
    for i in range(count):
        j = i + 1 if i % 2 == parity else i - 1
        if periodic or 0 <= j < count:
            pairs.append((i, j % count))
    return lax.ppermute(x, axis, pairs)


def local(
    nx,
    ny,
    zonal,
    merid,
    thick,
    land,
    visc,
    wind,
    gravity,
    conv_first,
    bias_first,
    conv_second,
    bias_second,
    conv_last,
):
    layers, columns, lat = zonal.shape
    big = pltpu.CompilerParams(vmem_limit_bytes=48 * 1024 * 1024)
    lon_rows = EDGE * FIELDS
    lat_a, lat_b = pl.pallas_call(
        pack_kernel,
        out_shape=[jax.ShapeDtypeStruct((columns, lat), BF16)] * 2,
        in_specs=[pl.BlockSpec(memory_space=pltpu.HBM)] * 6,
        out_specs=[VMEM] * 2,
        scratch_shapes=[pltpu.VMEM(a.shape, a.dtype) for a in (zonal, merid, thick, land, visc, wind)]
        + [pltpu.SemaphoreType.DMA] * 6,
        compiler_params=pltpu.CompilerParams(vmem_limit_bytes=62 * 1024 * 1024),
        name="pack",
    )(zonal, merid, thick, land, visc, wind)
    lat_a = swap(lat_a, "oy", 0, ny, False)
    lat_b = swap(lat_b, "oy", 1, ny, False)
    w1, w2, w3, b1, b2, grav = pl.pallas_call(
        weight_kernel,
        out_shape=[
            jax.ShapeDtypeStruct((4, 256, 256), BF16),
            jax.ShapeDtypeStruct((1024, 256), BF16),
            jax.ShapeDtypeStruct((2048, 128), BF16),
            jax.ShapeDtypeStruct((8, 256), F32),
            jax.ShapeDtypeStruct((8, 256), F32),
            jax.ShapeDtypeStruct((layers, 8, 2 * lat), F32),
        ],
        in_specs=[VMEM] * 6,
        out_specs=[VMEM] * 6,
        compiler_params=big,
        name="weights",
    )(conv_first, conv_second, conv_last, bias_first[None], bias_second[None], gravity[None])
    lon_a, lon_b = pl.pallas_call(
        lon_kernel,
        out_shape=[jax.ShapeDtypeStruct((lon_rows + 32, lat), BF16)] * 2,
        in_specs=[VMEM] * 8 + [pl.BlockSpec(memory_space=pl.ANY)],
        out_specs=[VMEM] * 2,
        compiler_params=big,
        name="lon",
    )(zonal, merid, thick, land, visc, wind, lat_a, lat_b, grav)
    lon_a = swap(lon_a, "ox", 0, nx, True)
    lon_b = swap(lon_b, "ox", 1, nx, True)
    wide = 2 * lat
    outer = columns + 4 * EDGE
    groups = columns // 8 + 1
    flow = jax.ShapeDtypeStruct((layers, columns, lat), F32)
    work = [
        pltpu.VMEM((FIELDS, outer, wide), F32),
        pltpu.VMEM((layers, outer, wide), F32),
        pltpu.VMEM((layers, outer, wide), F32),
        pltpu.VMEM((columns + 2 * EDGE, 16, wide), F32),
    ]
    zonal_mid, merid_mid, thick_mid, feat, edge_ext, edge_prs = pl.pallas_call(
        functools.partial(inner_kernel, ny),
        out_shape=[
            flow,
            flow,
            flow,
            jax.ShapeDtypeStruct((groups, PITCH, 256), BF16),
            jax.ShapeDtypeStruct((FIELDS, 32, wide), F32),
            jax.ShapeDtypeStruct((layers, 16, wide), F32),
        ],
        in_specs=[VMEM] * 9,
        out_specs=[VMEM] * 6,
        scratch_shapes=work,
        compiler_params=big,
        cost_estimate=pl.CostEstimate(flops=40_000_000, bytes_accessed=8_000_000, transcendentals=0),
        name="inner",
    )(zonal, merid, thick, land, visc, wind, grav, lat_a, lat_b)
    hbm = pl.BlockSpec(memory_space=pltpu.HBM)
    return pl.pallas_call(
        functools.partial(main_kernel, ny),
        out_shape=[flow] * 3 + [jax.ShapeDtypeStruct((columns, lat), F32)],
        in_specs=[hbm] * 3 + [VMEM] * 11,
        out_specs=[hbm] * 3 + [VMEM],
        input_output_aliases={0: 0, 1: 1, 2: 2},
        scratch_shapes=work
        + [
            pltpu.VMEM((4, PITCH, 256), BF16),
            pltpu.VMEM((groups, 4, PITCH, 256), BF16),
            pltpu.VMEM((groups, 4, PITCH, 256), BF16),
            pltpu.VMEM((columns // 2 + 1, PITCH, 256), BF16),
            pltpu.VMEM((8 * columns + 16, 128), F32),
            pltpu.VMEM((4 * columns, 128), F32),
            pltpu.VMEM((3, 2, layers, EDGE, lat), F32),
            pltpu.SemaphoreType.DMA((3, 2)),
        ],
        compiler_params=big,
        name="step",
    )(
        zonal_mid,
        merid_mid,
        thick_mid,
        grav,
        lon_a,
        lon_b,
        feat,
        edge_ext,
        edge_prs,
        w1,
        w2,
        w3,
        b1,
        b2,
    )


def solution(mesh):
    in_specs = (
        P(None, "ox", "oy"),
        P(None, "ox", "oy"),
        P(None, "ox", "oy"),
        P("ox", "oy"),
        P("ox", "oy"),
        P(None, "ox", "oy"),
        P(),
        P(),
        P(),
        P(),
        P(),
        P(),
    )
    out_specs = (P(None, "ox", "oy"), P(None, "ox", "oy"), P(None, "ox", "oy"), P("ox", "oy"))
    body = functools.partial(local, mesh.shape["ox"], mesh.shape["oy"])
    return jax.shard_map(body, mesh=mesh, in_specs=in_specs, out_specs=out_specs, check_vma=False)
```

```python
import functools

import jax
import jax.numpy as jnp
from jax import lax
from jax.experimental import pallas as pl
from jax.experimental.pallas import tpu as pltpu
from jax.sharding import PartitionSpec as P

TIME_STEP = 0.05
REST_DEPTH = 1.4
DRAG_RATE = 0.5

F32 = jnp.float32
BF16 = jnp.bfloat16
EDGE = 8
FIELDS = 16
PITCH = 80
VMEM = pl.BlockSpec(memory_space=pltpu.VMEM)


def slot(f):
    return 4 * (f % 4) + f // 4


def own_fields(zonal, merid, thick, land, visc, wind, rows):
    sea = land[rows, :].astype(F32)
    layers = zonal.shape[0]
    maps = [zonal[l, rows, :] * sea for l in range(layers)]
    maps += [merid[l, rows, :] * sea for l in range(layers)]
    maps += [thick[l, rows, :] - REST_DEPTH for l in range(layers)]
    return maps + [sea, visc[rows, :], wind[0, rows, :], wind[1, rows, :]]


def pack_kernel(*refs):
    sources, (lat_a, lat_b), held, sems = refs[:6], refs[6:8], refs[8:14], refs[14:]
    copies = [pltpu.make_async_copy(*each) for each in zip(sources, held, sems)]
    for copy in copies:
        copy.start()
    for copy in copies:
        copy.wait()
    zonal, merid, thick, land, visc, wind = held
    columns, lat = land.shape
    even_y = lax.rem(lax.axis_index("oy"), 2) == 0
    lane = lax.broadcasted_iota(jnp.int32, (16, lat), 1) // EDGE
    for c in range(0, columns, 16):
        low = jnp.zeros((16, lat), F32)
        high = jnp.zeros((16, lat), F32)
        for f, field in enumerate(own_fields(zonal, merid, thick, land, visc, wind, slice(c, c + 16))):
            here = lane == slot(f)
            low = jnp.where(here, pltpu.roll(field, EDGE * slot(f) % lat, 1), low)
            high = jnp.where(here, pltpu.roll(field, (EDGE * slot(f) + EDGE) % lat, 1), high)
        lat_a[c : c + 16, :] = jnp.where(even_y, high, low).astype(BF16)
        lat_b[c : c + 16, :] = jnp.where(even_y, low, high).astype(BF16)


def lon_kernel(zonal, merid, thick, land, visc, wind, got_a, got_b, after, lon_a, lon_b):
    del after
    columns = got_a.shape[0]
    even_x = lax.rem(lax.axis_index("ox"), 2) == 0
    size = EDGE * FIELDS
    maps_low = own_fields(zonal, merid, thick, land, visc, wind, slice(0, EDGE))
    maps_high = own_fields(zonal, merid, thick, land, visc, wind, slice(columns - EDGE, columns))
    for f in range(0, FIELDS, 2):
        low = jnp.concatenate(maps_low[f : f + 2], axis=0)
        high = jnp.concatenate(maps_high[f : f + 2], axis=0)
        lon_a[EDGE * f : EDGE * f + 16, :] = jnp.where(even_x, high, low).astype(BF16)
        lon_b[EDGE * f : EDGE * f + 16, :] = jnp.where(even_x, low, high).astype(BF16)
    for n, got in enumerate((got_a, got_b)):
        low = got[0:16, :]
        high = got[columns - 16 : columns, :]
        lon_a[size + 16 * n : size + 16 * n + 16, :] = jnp.where(even_x, high, low)
        lon_b[size + 16 * n : size + 16 * n + 16, :] = jnp.where(even_x, low, high)


def weight_kernel(first, second, last, bias_first, bias_second, gravity, w1, w2, w3, b1, b2, grav):
    hidden = second.shape[2]
    zero = jnp.zeros((hidden, hidden), F32)
    turned = [[second[a, b].astype(F32).T * 0.5 for b in range(3)] for a in range(3)]
    tap = lambda a, b: turned[a][b] if 0 <= a < 3 and 0 <= b < 3 else zero
    for px in range(4):
        for py in range(4):
            ex, ey, a, b = px % 2, py % 2, px // 2, py // 2
            row = ((2 * a + b) * 4 + 2 * ex + ey) * hidden
            for dx in range(2):
                w2[row : row + hidden, 128 * dx : 128 * dx + 128] = jnp.concatenate(
                    [tap(px - dx, py), tap(px - dx, py - 1)], axis=1
                ).astype(BF16)
    feats = first.shape[3]
    spot = lax.broadcasted_iota(jnp.int32, (256, feats), 0)
    chan = lax.broadcasted_iota(jnp.int32, (256, feats), 1)
    total = jnp.zeros((256, hidden), F32)
    ddx, ddy = spot // 128, (spot // 64) % 2
    for a in range(3):
        for b in range(3):
            want = ((ddx + a) * 4 + ddy + b) * feats + chan
            place = jnp.where(spot % 64 == want, 0.5, 0.0).astype(BF16)
            total = total + lax.dot_general(
                place, first[a, b], (((1,), (1,)), ((), ())), preferred_element_type=F32
            )
    base = jnp.concatenate(
        [
            jnp.concatenate([total[0:64], total[64:128]], axis=1),
            jnp.concatenate([total[128:192], total[192:256]], axis=1),
        ],
        axis=1,
    )
    for s in range(4):
        off = 80 + 32 * s
        w1[s] = jnp.concatenate(
            [jnp.zeros((off, 256), F32), base, jnp.zeros((192 - off, 256), F32)], axis=0
        ).astype(BF16)
    row = lax.broadcasted_iota(jnp.int32, (16, 128), 0)
    blank = jnp.zeros((1, hidden), F32)
    piece = lambda a, b: last[a, b].astype(F32) if 0 <= a < 3 and 0 <= b < 3 else blank
    for ex in range(2):
        tile = jnp.zeros((16, 128), F32)
        for k in range(16):
            a, dx, b, dy = k // 8, (k // 4) % 2, (k // 2) % 2, k % 2
            p, q = 2 * a + ex - dx, 2 * b - dy
            line = jnp.concatenate([piece(p, q), piece(p, q + 1)], axis=1)
            tile = jnp.where(row == k, jnp.broadcast_to(line, (16, 128)), tile)
        turned_tile = jnp.concatenate([tile] * 8, axis=0).T
        lane = lax.broadcasted_iota(jnp.int32, (128, 128), 1) // 16
        for m in range(8):
            start = 256 * m + 128 * ex
            w3[start : start + 128, :] = jnp.where(lane == m, turned_tile, 0.0).astype(BF16)
    for bias, out in ((bias_first, b1), (bias_second, b2)):
        half = bias[...] * 0.5
        out[...] = jnp.broadcast_to(jnp.concatenate([half] * 4, axis=1), (8, 256))
    for l in range(grav.shape[0]):
        grav[l] = jnp.broadcast_to(gravity[0:1, l : l + 1], grav.shape[1:])


def far_tile(n_rows, s_rows, f):
    lat = n_rows.shape[1]
    lane = lax.broadcasted_iota(jnp.int32, n_rows.shape, 1)
    up = pltpu.roll(n_rows, (lat - EDGE * slot(f)) % lat, 1)
    down = pltpu.roll(s_rows, (2 * lat - EDGE - EDGE * slot(f)) % lat, 1)
    return jnp.where(lane < EDGE, up, jnp.where(lane >= lat - EDGE, down, 0.0))


def dynamics(layers, wide, lat, lat_count, ext, nxt, prs, grav, store, emit):
    oy = lax.axis_index("oy")
    sea_id, visc_id, wind_id = 3 * layers, 3 * layers + 1, 3 * layers + 2
    place = lax.broadcasted_iota(jnp.int32, (EDGE, wide), 1)
    if wide > lat:
        place = jnp.where(place < lat + lat // 2, place, place - wide)
    coriolis = 0.3 + 1.4 * ((oy * lat + place).astype(F32) + 0.5) / (lat_count * lat)

    def up(x):
        return pltpu.roll(x, wide - 1, 1)

    def down(x):
        return pltpu.roll(x, 1, 1)

    def rows_of(ch):
        r = EDGE + EDGE * ch
        return slice(r, r + 8), slice(r + 1, r + 9), slice(r - 1, r + 7)

    def thickness(ch):
        here, plus, minus = rows_of(ch)
        sea = ext[sea_id, here, :]
        odd = []
        for l in range(layers):
            h = ext[2 * layers + l, here, :]
            flux_e = ext[l, plus, :] * ext[2 * layers + l, plus, :]
            flux_w = ext[l, minus, :] * ext[2 * layers + l, minus, :]
            flux_y = ext[layers + l, here, :] * h
            diverge = (flux_e - flux_w) * 0.5 + (up(flux_y) - down(flux_y)) * 0.5
            h = h - TIME_STEP * sea * diverge
            nxt[l, here, :] = h
            odd.append(h - REST_DEPTH)
        for l in reversed(range(layers - 1)):
            odd[l] = odd[l] + odd[l + 1]
        total = jnp.zeros_like(sea)
        for l in range(layers):
            total = total + grav[l, :, 0:wide] * odd[l]
            prs[l, here, :] = total

    def velocity(ch):
        here, plus, minus = rows_of(ch)
        sea = ext[sea_id, here, :]
        v = ext[visc_id, here, :]
        mix = [
            0.5 * (v + ext[visc_id, plus, :]),
            0.5 * (v + ext[visc_id, minus, :]),
            0.5 * (v + up(v)),
            0.5 * (v + down(v)),
        ]

        def lap(f, q):
            near = (ext[f, plus, :], ext[f, minus, :], up(q), down(q))
            total = mix[0] * (near[0] - q)
            for side in range(1, 4):
                total = total + mix[side] * (near[side] - q)
            return total

        heavy = jnp.zeros_like(sea)
        moving = jnp.zeros_like(sea)
        for l in range(layers):
            zm = ext[l, here, :]
            vm = ext[layers + l, here, :]
            p = prs[l, here, :]
            h = nxt[l, here, :]
            grad_x = (prs[l, plus, :] - prs[l, minus, :]) * 0.5
            grad_y = (up(p) - down(p)) * 0.5
            push_x = coriolis * vm - grad_x + lap(l, zm)
            push_y = -coriolis * zm - grad_y + lap(layers + l, vm)
            if l == 0:
                push_x = push_x + ext[wind_id, here, :] / h
                push_y = push_y + ext[wind_id + 1, here, :] / h
            if l == layers - 1:
                push_x = push_x - DRAG_RATE * zm
                push_y = push_y - DRAG_RATE * vm
            zn = sea * (zm + TIME_STEP * push_x)
            vn = sea * (vm + TIME_STEP * push_y)
            store(ch, l, zn[:, 0:lat], vn[:, 0:lat], h[:, 0:lat])
            heavy = heavy + h
            moving = moving + h * (zn * zn + vn * vn)
            if l == 0:
                maps = [zn, vn, sea * (h - REST_DEPTH)]
        maps.append(sea * (0.5 * moving / heavy))
        emit(ch, maps)

    return thickness, velocity


def block_features(spread, lat):
    wide = 2 * lat
    block = lax.broadcasted_iota(jnp.int32, (PITCH, wide), 0)
    source = lax.broadcasted_iota(jnp.int32, (PITCH, wide), 1)
    chooser = jnp.where(
        (block < lat // 2 + 2) & (source == lax.rem(wide - 3 + 2 * block, wide)), 1.0, 0.0
    ).astype(BF16)

    def take(t):
        got = spread[8 * t : 8 * t + 16].reshape(256, wide).astype(BF16)
        return lax.dot_general(
            chooser, got, (((1,), (1,)), ((), ())), preferred_element_type=F32
        ).astype(BF16)

    return take


def scatter(spread, row, maps, wide):
    for f, m in enumerate(maps):
        for dy in range(4):
            spread[row : row + m.shape[0], 4 * dy + f, :] = pltpu.roll(m, (wide - dy) % wide, 1) if dy else m


def own_kernel(
    lat_count,
    zonal,
    merid,
    thick,
    land,
    visc,
    wind,
    grav,
    zonal_own,
    merid_own,
    thick_own,
    energy_own,
    low_out,
    high_out,
    ext,
    nxt,
    prs,
):
    layers, columns, lat = zonal.shape
    base = 2 * EDGE
    group = lax.broadcasted_iota(jnp.int32, (EDGE, lat), 1) // EDGE
    for c in range(0, columns, EDGE):
        rows = slice(c, c + EDGE)
        low = jnp.zeros((EDGE, lat), F32)
        high = jnp.zeros((EDGE, lat), F32)
        for f, field in enumerate(own_fields(zonal, merid, thick, land, visc, wind, rows)):
            here = group == slot(f)
            low = jnp.where(here, pltpu.roll(field, EDGE * slot(f) % lat, 1), low)
            high = jnp.where(here, pltpu.roll(field, (EDGE * slot(f) + EDGE) % lat, 1), high)
            if 2 * layers <= f < 3 * layers:
                field = thick[f - 2 * layers, rows, :]
            ext[f, base + c : base + c + EDGE, :] = field
        low_out[rows, :] = low
        high_out[rows, :] = high

    def store(ch, l, zn, vn, h):
        row = EDGE * ch - EDGE
        zonal_own[l, row : row + 8, :] = zn
        merid_own[l, row : row + 8, :] = vn
        thick_own[l, row : row + 8, :] = h

    def emit(ch, maps):
        row = EDGE * ch - EDGE
        energy_own[row : row + 8, :] = maps[3]

    thickness, velocity = dynamics(layers, lat, lat, lat_count, ext, nxt, prs, grav, store, emit)
    own = columns // EDGE
    for ch in range(1, own + 1):
        thickness(ch)
    for ch in range(2, own):
        velocity(ch)


def inner_kernel(
    lat_count,
    zonal,
    merid,
    thick,
    land,
    visc,
    wind,
    grav,
    lat_a,
    lat_b,
    zonal_own,
    merid_own,
    thick_own,
    energy_own,
    low_own,
    high_own,
    zonal_out,
    merid_out,
    thick_out,
    feat,
    edge_ext,
    strip,
    nxt,
    prs,
    spread,
):
    layers, columns, lat = zonal.shape
    oy = lax.axis_index("oy")
    even_y = lax.rem(oy, 2) == 0
    base = 2 * EDGE
    wide = 2 * lat
    own = columns // EDGE
    part = lat // layers
    lane = lax.broadcasted_iota(jnp.int32, (EDGE, lat), 1)
    layer = lane // part
    spot = lane % part

    def turn(x, shift):
        return pltpu.roll(x, shift % lat, 1) if shift % lat else x

    edge_rows = {0: 0, 8: 8, 16: 16, columns - 24: 24, columns - 16: 32, columns - 8: 40}
    for c in range(0, columns, 16):
        got_a = lat_a[c : c + 16, :].astype(F32)
        got_b = lat_b[c : c + 16, :].astype(F32)
        n_both = jnp.where(even_y, got_a, got_b)
        s_both = jnp.where(even_y, got_b, got_a)
        for h in range(0, 16, EDGE):
            rows = slice(c + h, c + h + EDGE)
            north, south = n_both[h : h + EDGE], s_both[h : h + EDGE]
            low, high = low_own[rows, :], high_own[rows, :]
            four = []
            for g in range(4):
                tile = jnp.where(spot < 24, turn(high, 16 - 8 * g), turn(north, 24 - 8 * g))
                tile = jnp.where(spot < 16, turn(low, 8 - 8 * g), tile)
                four.append(jnp.where(spot < 8, turn(south, -8 * g), tile))
            four[2] = four[2] + REST_DEPTH
            other = four.pop()
            sea, v = other, turn(other, -part)
            for l in range(1, layers):
                sea = jnp.where(layer == l, turn(other, part * l), sea)
                v = jnp.where(layer == l, turn(other, part * (l - 1)), v)
            four += [sea, v, turn(other, -2 * part), turn(other, -3 * part)]
            row = base + c + h
            for n, tile in enumerate(four):
                strip[n, row : row + EDGE, :] = tile
            edge = edge_rows.get(c + h)
            if edge is not None:
                maps = own_fields(zonal, merid, thick, land, visc, wind, rows)
                for f in range(FIELDS):
                    lift = REST_DEPTH if 2 * layers <= f < 3 * layers else 0.0
                    first = thick[f - 2 * layers, rows, :] if lift else maps[f]
                    edge_ext[f, edge : edge + EDGE, 0:lat] = first
                    edge_ext[f, edge : edge + EDGE, lat:wide] = far_tile(north, south, f) + lift

    def lanes(rows):
        at = lax.broadcasted_iota(jnp.int32, (rows, lat), 1)
        return at, at // part, at % part

    up = lambda x: turn(x, -1)
    down = lambda x: turn(x, 1)

    some = columns // 1
    lane, layer, spot = lanes(some)
    pull = jnp.broadcast_to(grav[0, 0:1, 0:lat], (some, lat))
    for l in range(1, layers):
        pull = jnp.where(layer == l, jnp.broadcast_to(grav[l, 0:1, 0:lat], (some, lat)), pull)
    for r in range(base, base + columns, some):
        here, plus, minus = slice(r, r + some), slice(r + 1, r + some + 1), slice(r - 1, r + some - 1)
        h = strip[2, here, :]
        flux_y = strip[1, here, :] * h
        flux_e = strip[0, plus, :] * strip[2, plus, :]
        flux_w = strip[0, minus, :] * strip[2, minus, :]
        diverge = (flux_e - flux_w) * 0.5 + (up(flux_y) - down(flux_y)) * 0.5
        h = h - TIME_STEP * strip[3, here, :] * diverge
        nxt[here, :] = h
        total = h - REST_DEPTH
        total = total + jnp.where(layer < 3, turn(total, -part), 0.0)
        total = total + jnp.where(layer < 2, turn(total, -2 * part), 0.0)
        total = total * pull
        total = total + jnp.where(layer >= 1, turn(total, part), 0.0)
        prs[here, :] = total + jnp.where(layer >= 2, turn(total, 2 * part), 0.0)

    def over_layers(x):
        x = x + turn(x, part)
        return x + turn(x, 2 * part)

    def patch(tile, result, l):
        tile = jnp.where(lane < 2, turn(result, -EDGE - part * l), tile)
        return jnp.where(lane >= lat - 2, turn(result, lat - 24 - part * l), tile)

    some = (columns - 2 * EDGE) // 1
    lane, layer, spot = lanes(some)
    place = jnp.where(spot < 16, spot - EDGE, lat - EDGE + spot - 16)
    coriolis = 0.3 + 1.4 * ((oy * lat + place).astype(F32) + 0.5) / (lat_count * lat)
    drag = jnp.where(layer == layers - 1, DRAG_RATE, 0.0)
    for r in range(base + EDGE, base + columns - EDGE, some):
        here, plus, minus = slice(r, r + some), slice(r + 1, r + some + 1), slice(r - 1, r + some - 1)
        row = slice(r - base, r - base + some)
        v = strip[4, here, :]
        mix = [
            0.5 * (v + strip[4, plus, :]),
            0.5 * (v + strip[4, minus, :]),
            0.5 * (v + up(v)),
            0.5 * (v + down(v)),
        ]

        def lap(n, q):
            near = (strip[n, plus, :], strip[n, minus, :], up(q), down(q))
            total = mix[0] * (near[0] - q)
            for side in range(1, 4):
                total = total + mix[side] * (near[side] - q)
            return total

        sea = strip[3, here, :]
        zm, vm = strip[0, here, :], strip[1, here, :]
        h, p = nxt[here, :], prs[here, :]
        grad_x = (prs[plus, :] - prs[minus, :]) * 0.5
        grad_y = (up(p) - down(p)) * 0.5
        wind_x = jnp.where(layer == 0, strip[5, here, :] / h, 0.0)
        wind_y = jnp.where(layer == 0, strip[6, here, :] / h, 0.0)
        zn = sea * (zm + TIME_STEP * (coriolis * vm - grad_x + lap(0, zm) + wind_x - drag * zm))
        vn = sea * (vm + TIME_STEP * (-coriolis * zm - grad_y + lap(1, vm) + wind_y - drag * vm))
        energy = sea * (0.5 * over_layers(h * (zn * zn + vn * vn)) / over_layers(h))
        for l in range(layers):
            for source, result, out in (
                (zonal_own, zn, zonal_out),
                (merid_own, vn, merid_out),
                (thick_own, h, thick_out),
            ):
                out[l, row, :] = patch(source[l, row, :], result, l)
        own_sea = land[row, :].astype(F32)
        maps = []
        for tile, result in (
            (zonal_own[0, row, :], zn),
            (merid_own[0, row, :], vn),
            (own_sea * (thick_own[0, row, :] - REST_DEPTH), sea * (h - REST_DEPTH)),
            (energy_own[row, :], energy),
        ):
            far = jnp.where(lane < 3, turn(result, -24), jnp.where(lane >= lat - 3, turn(result, -8), 0.0))
            maps.append(jnp.concatenate([patch(tile, result, 0), far], axis=1))
        scatter(spread, r - EDGE, maps, wide)

    take = block_features(spread, lat)
    for t in range(2, own, 2):
        g = take(t)
        feat[t] = g
        feat[t + 1, :, 0:128] = g[:, 128:256]
        feat[t - 1, :, 128:256] = g[:, 0:128]


def main_kernel(
    lat_count,
    zonal_in,
    merid_in,
    thick_in,
    grav,
    lon_a,
    lon_b,
    inner_feat,
    edge_ext,
    w1,
    w2,
    w3,
    b1,
    b2,
    zonal_out,
    merid_out,
    thick_out,
    visc_out,
    ext,
    nxt,
    prs,
    spread,
    feat,
    act,
    act_up,
    second,
    parts,
    sums,
    edge_out,
    sems,
):
    columns, lat = visc_out.shape
    layers = grav.shape[0]
    oy = lax.axis_index("oy")
    even_y = lax.rem(oy, 2) == 0
    even_x = lax.rem(lax.axis_index("ox"), 2) == 0
    base = 2 * EDGE
    wide = 2 * lat
    own = columns // EDGE

    inside = pl.ds(EDGE, columns - 2 * EDGE)
    copies = [
        pltpu.make_async_copy(mid.at[:, inside, :], out.at[:, inside, :], sems.at[k, 2])
        for k, (mid, out) in enumerate(((zonal_in, zonal_out), (merid_in, merid_out), (thick_in, thick_out)))
    ]
    for copy in copies:
        copy.start()

    west = jnp.where(even_x, lon_b[...], lon_a[...])
    east = jnp.where(even_x, lon_a[...], lon_b[...])
    size = EDGE * FIELDS
    for side, slot, row in ((west, slice(8, 16), base - EDGE), (east, slice(0, 8), base + columns)):
        from_a = side[size : size + 16].astype(F32)[slot]
        from_b = side[size + 16 : size + 32].astype(F32)[slot]
        north = jnp.where(even_y, from_a, from_b)
        south = jnp.where(even_y, from_b, from_a)
        near = side[:size].astype(F32)
        for f in range(FIELDS):
            lift = REST_DEPTH if 2 * layers <= f < 3 * layers else 0.0
            ext[f, row : row + EDGE, 0:lat] = near[EDGE * f : EDGE * f + EDGE] + lift
            ext[f, row : row + EDGE, lat:wide] = far_tile(north, south, f) + lift
    for f in range(FIELDS):
        ext[f, base : base + 24, :] = edge_ext[f, 0:24, :]
        ext[f, base + columns - 24 : base + columns, :] = edge_ext[f, 24:48, :]

    def store(ch, l, zn, vn, h):
        if ch in (1, own):
            side = 0 if ch == 1 else 1
            for k, tile in enumerate((zn, vn, h)):
                edge_out[k, side, l] = tile

    place = lax.broadcasted_iota(jnp.int32, (EDGE, wide), 1)
    in_lat = (place < lat + 3) | (place >= wide - 3)

    def emit(ch, maps):
        column = lax.broadcasted_iota(jnp.int32, (EDGE, wide), 0) + (EDGE + EDGE * ch - base)
        keep = in_lat & (column >= -3) & (column < columns + 3)
        scatter(spread, EDGE * ch, [jnp.where(keep, m, 0.0) for m in maps], wide)

    thickness, velocity = dynamics(layers, wide, lat, lat_count, ext, nxt, prs, grav, store, emit)
    edges = (0, 1, own, own + 1)
    for ch in (0, 1, 2, own - 1, own, own + 1):
        thickness(ch)

    for ch in edges:
        velocity(ch)
    copies += [
        pltpu.make_async_copy(
            edge_out.at[k, side],
            out.at[:, pl.ds(side * (columns - EDGE), EDGE), :],
            sems.at[k, side],
        )
        for k, out in enumerate((zonal_out, merid_out, thick_out))
        for side in range(2)
    ]
    for copy in copies[3:]:
        copy.start()

    take = block_features(spread, lat)
    blocks = lat // 2 + 2
    first, last = take(0), take(own)
    feat[0] = first
    feat[1, :, 0:128] = first[:, 128:256]
    feat[1, :, 128:256] = inner_feat[1, :, 128:256]
    feat[2, :, 0:128] = inner_feat[own - 1, :, 0:128]
    feat[2, :, 128:256] = last[:, 0:128]
    feat[3] = last

    south_end = jnp.where(oy == 0, 0.0, 1.0)
    north_end = jnp.where(oy == lat_count - 1, 0.0, 1.0)
    brow = lax.broadcasted_iota(jnp.int32, (8, 256), 0)
    quad = lax.broadcasted_iota(jnp.int32, (8, 256), 1) // 64 % 2
    low_1 = jnp.where(brow == 0, south_end, 1.0)
    high_1 = jnp.where(brow == blocks - 1 - 64, north_end, 1.0)
    low_2 = jnp.where((brow == 0) & (quad == 0), south_end, 1.0)
    high_2 = jnp.where((brow == blocks - 2 - 64) & (quad == 1), north_end, 1.0)

    def activate(total, bias, count, low, high):
        total = total + bias
        total = total * jnp.tanh(total) + total
        total = total.reshape(count, PITCH, 256)
        return jnp.concatenate(
            [total[:, 0:8] * low, total[:, 8:64], total[:, 64:72] * high, total[:, 72:]], axis=1
        )

    bias1 = b1[0:1, :]
    bias2 = b2[0:1, :]
    groups = inner_feat.shape[0]

    def first_step(n, carry):
        left = jnp.concatenate([feat[0:2], inner_feat[2 : own - 1], feat[2:4]], axis=0).reshape(groups * PITCH, 256)
        h = jnp.dot(left, w1[n], preferred_element_type=F32)
        h = activate(h, bias1, groups, low_1, high_1)
        moved = pltpu.roll(h.reshape(groups * PITCH, 256), groups * PITCH - 1, 0)
        act[:, n] = h.astype(BF16)
        act_up[:, n] = moved.reshape(groups, PITCH, 256).astype(BF16)
        return carry

    lax.fori_loop(0, 4, first_step, 0)

    block_rows = columns // 2 + 1
    some = next(n for n in range(16, 0, -1) if block_rows % n == 0)
    flat = lambda ref: ref.reshape(4 * groups, PITCH, 256)
    first_act, first_up = flat(act), flat(act_up)

    def second_step(n, carry):
        at = n * some
        parts_of = [
            ref[pl.ds(at + shift, some)].reshape(some * PITCH, 256)
            for shift in range(2)
            for ref in (first_act, first_up)
        ]
        h = jnp.dot(jnp.concatenate(parts_of, axis=1), w2[...], preferred_element_type=F32)
        second[pl.ds(at, some)] = activate(h, bias2, some, low_2, high_2).astype(BF16)
        return carry

    lax.fori_loop(0, block_rows // some, second_step, 0)

    eights = columns // 16
    wide_left = [
        jnp.concatenate([second[8 * g + m] for g in range(eights)], axis=0) for m in range(8)
    ]
    total = jnp.dot(jnp.concatenate(wide_left, axis=1), w3[...], preferred_element_type=F32)
    pad = jnp.zeros((128 - PITCH, 128), F32)
    for g in range(eights):
        parts[128 * g : 128 * g + 128, :] = jnp.concatenate([total[PITCH * g : PITCH * (g + 1)], pad], axis=0).T
    end = jnp.dot(second[8 * eights], w3[0:256], preferred_element_type=F32)
    parts[128 * eights : 128 * eights + 16, :] = jnp.concatenate([end, pad], axis=0).T[0:16]

    for i in range(columns // 2):
        sums[8 * i : 8 * i + 8, :] = parts[16 * i : 16 * i + 8, :] + parts[16 * i + 24 : 16 * i + 32, :]
    jj = lax.broadcasted_iota(jnp.int32, (128, lat), 0)
    ll = lax.broadcasted_iota(jnp.int32, (128, lat), 1)
    out = jnp.zeros((columns, lat), F32)
    for k in range(4):
        x = sums[pl.ds(k, columns, stride=4), :]
        high = x.astype(BF16)
        rest = (x - high.astype(F32)).astype(BF16)
        put_at = jnp.where(ll == 2 * (jj - k // 2) + k % 2, 1.0, 0.0).astype(BF16)
        out = out + jnp.dot(high, put_at, preferred_element_type=F32)
        out = out + jnp.dot(rest, put_at, preferred_element_type=F32)
    visc_out[...] = jnp.exp(out)
    for copy in copies:
        copy.wait()


def swap(x, axis, parity, count, periodic):
    pairs = []
    for i in range(count):
        j = i + 1 if i % 2 == parity else i - 1
        if periodic or 0 <= j < count:
            pairs.append((i, j % count))
    return lax.ppermute(x, axis, pairs)


def local(
    nx,
    ny,
    zonal,
    merid,
    thick,
    land,
    visc,
    wind,
    gravity,
    conv_first,
    bias_first,
    conv_second,
    bias_second,
    conv_last,
):
    layers, columns, lat = zonal.shape
    big = pltpu.CompilerParams(vmem_limit_bytes=48 * 1024 * 1024)
    lon_rows = EDGE * FIELDS
    lat_a, lat_b = pl.pallas_call(
        pack_kernel,
        out_shape=[jax.ShapeDtypeStruct((columns, lat), BF16)] * 2,
        in_specs=[pl.BlockSpec(memory_space=pltpu.HBM)] * 6,
        out_specs=[VMEM] * 2,
        scratch_shapes=[pltpu.VMEM(a.shape, a.dtype) for a in (zonal, merid, thick, land, visc, wind)]
        + [pltpu.SemaphoreType.DMA] * 6,
        compiler_params=pltpu.CompilerParams(vmem_limit_bytes=62 * 1024 * 1024),
        name="pack",
    )(zonal, merid, thick, land, visc, wind)
    lat_a = swap(lat_a, "oy", 0, ny, False)
    lat_b = swap(lat_b, "oy", 1, ny, False)
    w1, w2, w3, b1, b2, grav = pl.pallas_call(
        weight_kernel,
        out_shape=[
            jax.ShapeDtypeStruct((4, 256, 256), BF16),
            jax.ShapeDtypeStruct((1024, 256), BF16),
            jax.ShapeDtypeStruct((2048, 128), BF16),
            jax.ShapeDtypeStruct((8, 256), F32),
            jax.ShapeDtypeStruct((8, 256), F32),
            jax.ShapeDtypeStruct((layers, 8, 2 * lat), F32),
        ],
        in_specs=[VMEM] * 6,
        out_specs=[VMEM] * 6,
        compiler_params=big,
        name="weights",
    )(conv_first, conv_second, conv_last, bias_first[None], bias_second[None], gravity[None])
    flow = jax.ShapeDtypeStruct((layers, columns, lat), F32)
    flat = jax.ShapeDtypeStruct((columns, lat), F32)
    outer = columns + 4 * EDGE
    inputs = (zonal, merid, thick, land, visc, wind)
    own = pl.pallas_call(
        functools.partial(own_kernel, ny),
        out_shape=[flow] * 3 + [flat] * 3,
        in_specs=[VMEM] * 7,
        out_specs=[VMEM] * 6,
        scratch_shapes=[
            pltpu.VMEM((FIELDS, outer, lat), F32),
            pltpu.VMEM((layers, outer, lat), F32),
            pltpu.VMEM((layers, outer, lat), F32),
        ],
        compiler_params=big,
        cost_estimate=pl.CostEstimate(flops=20_000_000, bytes_accessed=4_000_000, transcendentals=0),
        name="own",
    )(*inputs, grav)
    lon_a, lon_b = pl.pallas_call(
        lon_kernel,
        out_shape=[jax.ShapeDtypeStruct((lon_rows + 32, lat), BF16)] * 2,
        in_specs=[VMEM] * 8 + [pl.BlockSpec(memory_space=pl.ANY)],
        out_specs=[VMEM] * 2,
        compiler_params=big,
        name="lon",
    )(*inputs, lat_a, lat_b, own[3])
    lon_a = swap(lon_a, "ox", 0, nx, True)
    lon_b = swap(lon_b, "ox", 1, nx, True)
    wide = 2 * lat
    groups = columns // 8 + 1
    work = [
        pltpu.VMEM((FIELDS, outer, wide), F32),
        pltpu.VMEM((layers, outer, wide), F32),
        pltpu.VMEM((layers, outer, wide), F32),
        pltpu.VMEM((columns + 2 * EDGE, 16, wide), F32),
    ]
    zonal_mid, merid_mid, thick_mid, feat, edge_ext = pl.pallas_call(
        functools.partial(inner_kernel, ny),
        out_shape=[
            flow,
            flow,
            flow,
            jax.ShapeDtypeStruct((groups, PITCH, 256), BF16),
            jax.ShapeDtypeStruct((FIELDS, 48, wide), F32),
        ],
        in_specs=[VMEM] * 15,
        out_specs=[VMEM] * 5,
        scratch_shapes=[
            pltpu.VMEM((7, outer, lat), F32),
            pltpu.VMEM((outer, lat), F32),
            pltpu.VMEM((outer, lat), F32),
            pltpu.VMEM((columns + 2 * EDGE, 16, wide), F32),
        ],
        compiler_params=big,
        cost_estimate=pl.CostEstimate(flops=40_000_000, bytes_accessed=8_000_000, transcendentals=0),
        name="inner",
    )(*inputs, grav, lat_a, lat_b, *own)
    hbm = pl.BlockSpec(memory_space=pltpu.HBM)
    return pl.pallas_call(
        functools.partial(main_kernel, ny),
        out_shape=[flow] * 3 + [jax.ShapeDtypeStruct((columns, lat), F32)],
        in_specs=[VMEM] * 13,
        out_specs=[hbm] * 3 + [VMEM],
        scratch_shapes=work
        + [
            pltpu.VMEM((4, PITCH, 256), BF16),
            pltpu.VMEM((groups, 4, PITCH, 256), BF16),
            pltpu.VMEM((groups, 4, PITCH, 256), BF16),
            pltpu.VMEM((columns // 2 + 1, PITCH, 256), BF16),
            pltpu.VMEM((8 * columns + 16, 128), F32),
            pltpu.VMEM((4 * columns, 128), F32),
            pltpu.VMEM((3, 2, layers, EDGE, lat), F32),
            pltpu.SemaphoreType.DMA((3, 3)),
        ],
        compiler_params=big,
        name="step",
    )(
        zonal_mid,
        merid_mid,
        thick_mid,
        grav,
        lon_a,
        lon_b,
        feat,
        edge_ext,
        w1,
        w2,
        w3,
        b1,
        b2,
    )


def solution(mesh):
    in_specs = (
        P(None, "ox", "oy"),
        P(None, "ox", "oy"),
        P(None, "ox", "oy"),
        P("ox", "oy"),
        P("ox", "oy"),
        P(None, "ox", "oy"),
        P(),
        P(),
        P(),
        P(),
        P(),
        P(),
    )
    out_specs = (P(None, "ox", "oy"), P(None, "ox", "oy"), P(None, "ox", "oy"), P("ox", "oy"))
    body = functools.partial(local, mesh.shape["ox"], mesh.shape["oy"])
    return jax.shard_map(body, mesh=mesh, in_specs=in_specs, out_specs=out_specs, check_vma=False)
```

```python
import functools

import jax
import jax.numpy as jnp
from jax import lax
from jax.experimental import pallas as pl
from jax.experimental.pallas import tpu as pltpu
from jax.sharding import PartitionSpec as P

TIME_STEP = 0.05
REST_DEPTH = 1.4
DRAG_RATE = 0.5

F32 = jnp.float32
BF16 = jnp.bfloat16
EDGE = 8
FIELDS = 16
PITCH = 80
VMEM = pl.BlockSpec(memory_space=pltpu.VMEM)


def slot(f):
    return 4 * (f % 4) + f // 4


def own_fields(zonal, merid, thick, land, visc, wind, rows):
    sea = land[rows, :].astype(F32)
    layers = zonal.shape[0]
    maps = [zonal[l, rows, :] * sea for l in range(layers)]
    maps += [merid[l, rows, :] * sea for l in range(layers)]
    maps += [thick[l, rows, :] - REST_DEPTH for l in range(layers)]
    return maps + [sea, visc[rows, :], wind[0, rows, :], wind[1, rows, :]]


def pack_kernel(*refs):
    sources, (lat_a, lat_b), held, sems = refs[:6], refs[6:8], refs[8:14], refs[14:]
    copies = [pltpu.make_async_copy(*each) for each in zip(sources, held, sems)]
    for copy in copies:
        copy.start()
    for copy in copies:
        copy.wait()
    zonal, merid, thick, land, visc, wind = held
    columns, lat = land.shape
    even_y = lax.rem(lax.axis_index("oy"), 2) == 0
    lane = lax.broadcasted_iota(jnp.int32, (16, lat), 1) // EDGE
    for c in range(0, columns, 16):
        low = jnp.zeros((16, lat), F32)
        high = jnp.zeros((16, lat), F32)
        for f, field in enumerate(own_fields(zonal, merid, thick, land, visc, wind, slice(c, c + 16))):
            here = lane == slot(f)
            low = jnp.where(here, pltpu.roll(field, EDGE * slot(f) % lat, 1), low)
            high = jnp.where(here, pltpu.roll(field, (EDGE * slot(f) + EDGE) % lat, 1), high)
        lat_a[c : c + 16, :] = jnp.where(even_y, high, low).astype(BF16)
        lat_b[c : c + 16, :] = jnp.where(even_y, low, high).astype(BF16)


def lon_kernel(zonal, merid, thick, land, visc, wind, got_a, got_b, after, lon_a, lon_b):
    del after
    columns = got_a.shape[0]
    even_x = lax.rem(lax.axis_index("ox"), 2) == 0
    size = EDGE * FIELDS
    maps_low = own_fields(zonal, merid, thick, land, visc, wind, slice(0, EDGE))
    maps_high = own_fields(zonal, merid, thick, land, visc, wind, slice(columns - EDGE, columns))
    for f in range(0, FIELDS, 2):
        low = jnp.concatenate(maps_low[f : f + 2], axis=0)
        high = jnp.concatenate(maps_high[f : f + 2], axis=0)
        lon_a[EDGE * f : EDGE * f + 16, :] = jnp.where(even_x, high, low).astype(BF16)
        lon_b[EDGE * f : EDGE * f + 16, :] = jnp.where(even_x, low, high).astype(BF16)
    for n, got in enumerate((got_a, got_b)):
        low = got[0:16, :]
        high = got[columns - 16 : columns, :]
        lon_a[size + 16 * n : size + 16 * n + 16, :] = jnp.where(even_x, high, low)
        lon_b[size + 16 * n : size + 16 * n + 16, :] = jnp.where(even_x, low, high)


def weight_kernel(first, second, last, bias_first, bias_second, gravity, w1, w2, w3, b1, b2, grav):
    hidden = second.shape[2]
    zero = jnp.zeros((hidden, hidden), F32)
    turned = [[second[a, b].astype(F32).T * 0.5 for b in range(3)] for a in range(3)]
    tap = lambda a, b: turned[a][b] if 0 <= a < 3 and 0 <= b < 3 else zero
    for px in range(4):
        for py in range(4):
            ex, ey, a, b = px % 2, py % 2, px // 2, py // 2
            row = ((2 * a + b) * 4 + 2 * ex + ey) * hidden
            for dx in range(2):
                w2[row : row + hidden, 128 * dx : 128 * dx + 128] = jnp.concatenate(
                    [tap(px - dx, py), tap(px - dx, py - 1)], axis=1
                ).astype(BF16)
    feats = first.shape[3]
    spot = lax.broadcasted_iota(jnp.int32, (256, feats), 0)
    chan = lax.broadcasted_iota(jnp.int32, (256, feats), 1)
    total = jnp.zeros((256, hidden), F32)
    ddx, ddy = spot // 128, (spot // 64) % 2
    for a in range(3):
        for b in range(3):
            want = ((ddx + a) * 4 + ddy + b) * feats + chan
            place = jnp.where(spot % 64 == want, 0.5, 0.0).astype(BF16)
            total = total + lax.dot_general(
                place, first[a, b], (((1,), (1,)), ((), ())), preferred_element_type=F32
            )
    base = jnp.concatenate(
        [
            jnp.concatenate([total[0:64], total[64:128]], axis=1),
            jnp.concatenate([total[128:192], total[192:256]], axis=1),
        ],
        axis=1,
    )
    for s in range(4):
        off = 80 + 32 * s
        w1[s] = jnp.concatenate(
            [jnp.zeros((off, 256), F32), base, jnp.zeros((192 - off, 256), F32)], axis=0
        ).astype(BF16)
    row = lax.broadcasted_iota(jnp.int32, (16, 128), 0)
    blank = jnp.zeros((1, hidden), F32)
    piece = lambda a, b: last[a, b].astype(F32) if 0 <= a < 3 and 0 <= b < 3 else blank
    for ex in range(2):
        tile = jnp.zeros((16, 128), F32)
        for k in range(16):
            a, dx, b, dy = k // 8, (k // 4) % 2, (k // 2) % 2, k % 2
            p, q = 2 * a + ex - dx, 2 * b - dy
            line = jnp.concatenate([piece(p, q), piece(p, q + 1)], axis=1)
            tile = jnp.where(row == k, jnp.broadcast_to(line, (16, 128)), tile)
        turned_tile = jnp.concatenate([tile] * 8, axis=0).T
        lane = lax.broadcasted_iota(jnp.int32, (128, 128), 1) // 16
        for m in range(8):
            start = 256 * m + 128 * ex
            w3[start : start + 128, :] = jnp.where(lane == m, turned_tile, 0.0).astype(BF16)
    for bias, out in ((bias_first, b1), (bias_second, b2)):
        half = bias[...] * 0.5
        out[...] = jnp.broadcast_to(jnp.concatenate([half] * 4, axis=1), (8, 256))
    for l in range(grav.shape[0]):
        grav[l] = jnp.broadcast_to(gravity[0:1, l : l + 1], grav.shape[1:])


def far_tile(n_rows, s_rows, f):
    lat = n_rows.shape[1]
    lane = lax.broadcasted_iota(jnp.int32, n_rows.shape, 1)
    up = pltpu.roll(n_rows, (lat - EDGE * slot(f)) % lat, 1)
    down = pltpu.roll(s_rows, (2 * lat - EDGE - EDGE * slot(f)) % lat, 1)
    return jnp.where(lane < EDGE, up, jnp.where(lane >= lat - EDGE, down, 0.0))


def dynamics(layers, wide, lat, lat_count, ext, nxt, prs, grav, store, emit):
    oy = lax.axis_index("oy")
    sea_id, visc_id, wind_id = 3 * layers, 3 * layers + 1, 3 * layers + 2
    place = lax.broadcasted_iota(jnp.int32, (EDGE, wide), 1)
    if wide > lat:
        place = jnp.where(place < lat + lat // 2, place, place - wide)
    coriolis = 0.3 + 1.4 * ((oy * lat + place).astype(F32) + 0.5) / (lat_count * lat)

    def up(x):
        return pltpu.roll(x, wide - 1, 1)

    def down(x):
        return pltpu.roll(x, 1, 1)

    def rows_of(ch):
        r = EDGE + EDGE * ch
        return slice(r, r + 8), slice(r + 1, r + 9), slice(r - 1, r + 7)

    def thickness(ch):
        here, plus, minus = rows_of(ch)
        sea = ext[sea_id, here, :]
        odd = []
        for l in range(layers):
            h = ext[2 * layers + l, here, :]
            flux_e = ext[l, plus, :] * ext[2 * layers + l, plus, :]
            flux_w = ext[l, minus, :] * ext[2 * layers + l, minus, :]
            flux_y = ext[layers + l, here, :] * h
            diverge = (flux_e - flux_w) * 0.5 + (up(flux_y) - down(flux_y)) * 0.5
            h = h - TIME_STEP * sea * diverge
            nxt[l, here, :] = h
            odd.append(h - REST_DEPTH)
        for l in reversed(range(layers - 1)):
            odd[l] = odd[l] + odd[l + 1]
        total = jnp.zeros_like(sea)
        for l in range(layers):
            total = total + grav[l, :, 0:wide] * odd[l]
            prs[l, here, :] = total

    def velocity(ch):
        here, plus, minus = rows_of(ch)
        sea = ext[sea_id, here, :]
        v = ext[visc_id, here, :]
        mix = [
            0.5 * (v + ext[visc_id, plus, :]),
            0.5 * (v + ext[visc_id, minus, :]),
            0.5 * (v + up(v)),
            0.5 * (v + down(v)),
        ]

        def lap(f, q):
            near = (ext[f, plus, :], ext[f, minus, :], up(q), down(q))
            total = mix[0] * (near[0] - q)
            for side in range(1, 4):
                total = total + mix[side] * (near[side] - q)
            return total

        heavy = jnp.zeros_like(sea)
        moving = jnp.zeros_like(sea)
        for l in range(layers):
            zm = ext[l, here, :]
            vm = ext[layers + l, here, :]
            p = prs[l, here, :]
            h = nxt[l, here, :]
            grad_x = (prs[l, plus, :] - prs[l, minus, :]) * 0.5
            grad_y = (up(p) - down(p)) * 0.5
            push_x = coriolis * vm - grad_x + lap(l, zm)
            push_y = -coriolis * zm - grad_y + lap(layers + l, vm)
            if l == 0:
                push_x = push_x + ext[wind_id, here, :] / h
                push_y = push_y + ext[wind_id + 1, here, :] / h
            if l == layers - 1:
                push_x = push_x - DRAG_RATE * zm
                push_y = push_y - DRAG_RATE * vm
            zn = sea * (zm + TIME_STEP * push_x)
            vn = sea * (vm + TIME_STEP * push_y)
            store(ch, l, zn[:, 0:lat], vn[:, 0:lat], h[:, 0:lat])
            heavy = heavy + h
            moving = moving + h * (zn * zn + vn * vn)
            if l == 0:
                maps = [zn, vn, sea * (h - REST_DEPTH)]
        maps.append(sea * (0.5 * moving / heavy))
        emit(ch, maps)

    return thickness, velocity


def block_features(spread, lat):
    wide = 2 * lat
    block = lax.broadcasted_iota(jnp.int32, (PITCH, wide), 0)
    source = lax.broadcasted_iota(jnp.int32, (PITCH, wide), 1)
    chooser = jnp.where(
        (block < lat // 2 + 2) & (source == lax.rem(wide - 3 + 2 * block, wide)), 1.0, 0.0
    ).astype(BF16)

    def take(t):
        got = spread[8 * t : 8 * t + 16].reshape(256, wide).astype(BF16)
        return lax.dot_general(
            chooser, got, (((1,), (1,)), ((), ())), preferred_element_type=F32
        ).astype(BF16)

    return take


def scatter(spread, row, maps, wide):
    for f, m in enumerate(maps):
        for dy in range(4):
            spread[row : row + m.shape[0], 4 * dy + f, :] = pltpu.roll(m, (wide - dy) % wide, 1) if dy else m


def own_kernel(
    lat_count,
    zonal,
    merid,
    thick,
    land,
    visc,
    wind,
    grav,
    zonal_own,
    merid_own,
    thick_own,
    energy_own,
    low_out,
    high_out,
    ext,
    nxt,
    prs,
):
    layers, columns, lat = zonal.shape
    base = 2 * EDGE
    group = lax.broadcasted_iota(jnp.int32, (EDGE, lat), 1) // EDGE
    for c in range(0, columns, EDGE):
        rows = slice(c, c + EDGE)
        low = jnp.zeros((EDGE, lat), F32)
        high = jnp.zeros((EDGE, lat), F32)
        for f, field in enumerate(own_fields(zonal, merid, thick, land, visc, wind, rows)):
            here = group == slot(f)
            low = jnp.where(here, pltpu.roll(field, EDGE * slot(f) % lat, 1), low)
            high = jnp.where(here, pltpu.roll(field, (EDGE * slot(f) + EDGE) % lat, 1), high)
            if 2 * layers <= f < 3 * layers:
                field = thick[f - 2 * layers, rows, :]
            ext[f, base + c : base + c + EDGE, :] = field
        low_out[rows, :] = low
        high_out[rows, :] = high

    def store(ch, l, zn, vn, h):
        row = EDGE * ch - EDGE
        zonal_own[l, row : row + 8, :] = zn
        merid_own[l, row : row + 8, :] = vn
        thick_own[l, row : row + 8, :] = h

    def emit(ch, maps):
        row = EDGE * ch - EDGE
        energy_own[row : row + 8, :] = maps[3]

    thickness, velocity = dynamics(layers, lat, lat, lat_count, ext, nxt, prs, grav, store, emit)
    own = columns // EDGE
    for ch in range(1, own + 1):
        thickness(ch)
    for ch in range(2, own):
        velocity(ch)


def inner_kernel(
    lat_count,
    zonal,
    merid,
    thick,
    land,
    visc,
    wind,
    grav,
    lat_a,
    lat_b,
    zonal_own,
    merid_own,
    thick_own,
    energy_own,
    low_own,
    high_own,
    zonal_out,
    merid_out,
    thick_out,
    feat,
    edge_ext,
    strip,
    nxt,
    prs,
    spread,
):
    layers, columns, lat = zonal.shape
    oy = lax.axis_index("oy")
    even_y = lax.rem(oy, 2) == 0
    base = 2 * EDGE
    wide = 2 * lat
    own = columns // EDGE
    part = lat // layers
    lane = lax.broadcasted_iota(jnp.int32, (EDGE, lat), 1)
    layer = lane // part
    spot = lane % part

    def turn(x, shift):
        return pltpu.roll(x, shift % lat, 1) if shift % lat else x

    edge_rows = {0: 0, 8: 8, 16: 16, columns - 24: 24, columns - 16: 32, columns - 8: 40}
    for c in range(0, columns, 16):
        got_a = lat_a[c : c + 16, :].astype(F32)
        got_b = lat_b[c : c + 16, :].astype(F32)
        n_both = jnp.where(even_y, got_a, got_b)
        s_both = jnp.where(even_y, got_b, got_a)
        for h in range(0, 16, EDGE):
            rows = slice(c + h, c + h + EDGE)
            north, south = n_both[h : h + EDGE], s_both[h : h + EDGE]
            low, high = low_own[rows, :], high_own[rows, :]
            four = []
            for g in range(4):
                tile = jnp.where(spot < 24, turn(high, 16 - 8 * g), turn(north, 24 - 8 * g))
                tile = jnp.where(spot < 16, turn(low, 8 - 8 * g), tile)
                four.append(jnp.where(spot < 8, turn(south, -8 * g), tile))
            four[2] = four[2] + REST_DEPTH
            other = four.pop()
            sea, v = other, turn(other, -part)
            for l in range(1, layers):
                sea = jnp.where(layer == l, turn(other, part * l), sea)
                v = jnp.where(layer == l, turn(other, part * (l - 1)), v)
            four += [sea, v, turn(other, -2 * part), turn(other, -3 * part)]
            row = base + c + h
            for n, tile in enumerate(four):
                strip[n, row : row + EDGE, :] = tile
            edge = edge_rows.get(c + h)
            if edge is not None:
                maps = own_fields(zonal, merid, thick, land, visc, wind, rows)
                for f in range(FIELDS):
                    lift = REST_DEPTH if 2 * layers <= f < 3 * layers else 0.0
                    first = thick[f - 2 * layers, rows, :] if lift else maps[f]
                    edge_ext[f, edge : edge + EDGE, 0:lat] = first
                    edge_ext[f, edge : edge + EDGE, lat:wide] = far_tile(north, south, f) + lift

    def lanes(rows):
        at = lax.broadcasted_iota(jnp.int32, (rows, lat), 1)
        return at, at // part, at % part

    up = lambda x: turn(x, -1)
    down = lambda x: turn(x, 1)

    some = columns // 1
    lane, layer, spot = lanes(some)
    pull = jnp.broadcast_to(grav[0, 0:1, 0:lat], (some, lat))
    for l in range(1, layers):
        pull = jnp.where(layer == l, jnp.broadcast_to(grav[l, 0:1, 0:lat], (some, lat)), pull)
    for r in range(base, base + columns, some):
        here, plus, minus = slice(r, r + some), slice(r + 1, r + some + 1), slice(r - 1, r + some - 1)
        h = strip[2, here, :]
        flux_y = strip[1, here, :] * h
        flux_e = strip[0, plus, :] * strip[2, plus, :]
        flux_w = strip[0, minus, :] * strip[2, minus, :]
        diverge = (flux_e - flux_w) * 0.5 + (up(flux_y) - down(flux_y)) * 0.5
        h = h - TIME_STEP * strip[3, here, :] * diverge
        nxt[here, :] = h
        total = h - REST_DEPTH
        total = total + jnp.where(layer < 3, turn(total, -part), 0.0)
        total = total + jnp.where(layer < 2, turn(total, -2 * part), 0.0)
        total = total * pull
        total = total + jnp.where(layer >= 1, turn(total, part), 0.0)
        prs[here, :] = total + jnp.where(layer >= 2, turn(total, 2 * part), 0.0)

    def over_layers(x):
        x = x + turn(x, part)
        return x + turn(x, 2 * part)

    def patch(tile, result, l):
        tile = jnp.where(lane < 2, turn(result, -EDGE - part * l), tile)
        return jnp.where(lane >= lat - 2, turn(result, lat - 24 - part * l), tile)

    some = (columns - 2 * EDGE) // 1
    lane, layer, spot = lanes(some)
    place = jnp.where(spot < 16, spot - EDGE, lat - EDGE + spot - 16)
    coriolis = 0.3 + 1.4 * ((oy * lat + place).astype(F32) + 0.5) / (lat_count * lat)
    drag = jnp.where(layer == layers - 1, DRAG_RATE, 0.0)
    for r in range(base + EDGE, base + columns - EDGE, some):
        here, plus, minus = slice(r, r + some), slice(r + 1, r + some + 1), slice(r - 1, r + some - 1)
        row = slice(r - base, r - base + some)
        v = strip[4, here, :]
        mix = [
            0.5 * (v + strip[4, plus, :]),
            0.5 * (v + strip[4, minus, :]),
            0.5 * (v + up(v)),
            0.5 * (v + down(v)),
        ]

        def lap(n, q):
            near = (strip[n, plus, :], strip[n, minus, :], up(q), down(q))
            total = mix[0] * (near[0] - q)
            for side in range(1, 4):
                total = total + mix[side] * (near[side] - q)
            return total

        sea = strip[3, here, :]
        zm, vm = strip[0, here, :], strip[1, here, :]
        h, p = nxt[here, :], prs[here, :]
        grad_x = (prs[plus, :] - prs[minus, :]) * 0.5
        grad_y = (up(p) - down(p)) * 0.5
        wind_x = jnp.where(layer == 0, strip[5, here, :] / h, 0.0)
        wind_y = jnp.where(layer == 0, strip[6, here, :] / h, 0.0)
        zn = sea * (zm + TIME_STEP * (coriolis * vm - grad_x + lap(0, zm) + wind_x - drag * zm))
        vn = sea * (vm + TIME_STEP * (-coriolis * zm - grad_y + lap(1, vm) + wind_y - drag * vm))
        energy = sea * (0.5 * over_layers(h * (zn * zn + vn * vn)) / over_layers(h))
        for l in range(layers):
            for source, result, out in (
                (zonal_own, zn, zonal_out),
                (merid_own, vn, merid_out),
                (thick_own, h, thick_out),
            ):
                out[l, row, :] = patch(source[l, row, :], result, l)
        own_sea = land[row, :].astype(F32)
        maps = []
        for tile, result in (
            (zonal_own[0, row, :], zn),
            (merid_own[0, row, :], vn),
            (own_sea * (thick_own[0, row, :] - REST_DEPTH), sea * (h - REST_DEPTH)),
            (energy_own[row, :], energy),
        ):
            far = jnp.where(lane < 3, turn(result, -24), jnp.where(lane >= lat - 3, turn(result, -8), 0.0))
            maps.append(jnp.concatenate([patch(tile, result, 0), far], axis=1))
        scatter(spread, r - EDGE, maps, wide)

    take = block_features(spread, lat)
    for t in range(2, own, 2):
        g = take(t)
        feat[t] = g
        feat[t + 1, :, 0:128] = g[:, 128:256]
        feat[t - 1, :, 128:256] = g[:, 0:128]


def main_kernel(
    lat_count,
    zonal_in,
    merid_in,
    thick_in,
    grav,
    lon_a,
    lon_b,
    inner_feat,
    edge_ext,
    w1,
    w2,
    w3,
    b1,
    b2,
    zonal_out,
    merid_out,
    thick_out,
    visc_out,
    ext,
    nxt,
    prs,
    spread,
    feat,
    act,
    act_up,
    second,
    parts,
    sums,
    edge_out,
    sems,
):
    columns, lat = visc_out.shape
    layers = grav.shape[0]
    oy = lax.axis_index("oy")
    even_y = lax.rem(oy, 2) == 0
    even_x = lax.rem(lax.axis_index("ox"), 2) == 0
    base = 2 * EDGE
    wide = 2 * lat
    own = columns // EDGE

    inside = pl.ds(EDGE, columns - 2 * EDGE)
    copies = [
        pltpu.make_async_copy(mid.at[:, inside, :], out.at[:, inside, :], sems.at[k, 2])
        for k, (mid, out) in enumerate(((zonal_in, zonal_out), (merid_in, merid_out), (thick_in, thick_out)))
    ]
    for copy in copies:
        copy.start()

    west = jnp.where(even_x, lon_b[...], lon_a[...])
    east = jnp.where(even_x, lon_a[...], lon_b[...])
    size = EDGE * FIELDS
    for side, slot, row in ((west, slice(8, 16), base - EDGE), (east, slice(0, 8), base + columns)):
        from_a = side[size : size + 16].astype(F32)[slot]
        from_b = side[size + 16 : size + 32].astype(F32)[slot]
        north = jnp.where(even_y, from_a, from_b)
        south = jnp.where(even_y, from_b, from_a)
        near = side[:size].astype(F32)
        for f in range(FIELDS):
            lift = REST_DEPTH if 2 * layers <= f < 3 * layers else 0.0
            ext[f, row : row + EDGE, 0:lat] = near[EDGE * f : EDGE * f + EDGE] + lift
            ext[f, row : row + EDGE, lat:wide] = far_tile(north, south, f) + lift
    for f in range(FIELDS):
        ext[f, base : base + 24, :] = edge_ext[f, 0:24, :]
        ext[f, base + columns - 24 : base + columns, :] = edge_ext[f, 24:48, :]

    def store(ch, l, zn, vn, h):
        if ch in (1, own):
            side = 0 if ch == 1 else 1
            for k, tile in enumerate((zn, vn, h)):
                edge_out[k, side, l] = tile

    place = lax.broadcasted_iota(jnp.int32, (EDGE, wide), 1)
    in_lat = (place < lat + 3) | (place >= wide - 3)

    def emit(ch, maps):
        column = lax.broadcasted_iota(jnp.int32, (EDGE, wide), 0) + (EDGE + EDGE * ch - base)
        keep = in_lat & (column >= -3) & (column < columns + 3)
        scatter(spread, EDGE * ch, [jnp.where(keep, m, 0.0) for m in maps], wide)

    thickness, velocity = dynamics(layers, wide, lat, lat_count, ext, nxt, prs, grav, store, emit)
    edges = (0, 1, own, own + 1)
    for ch in (0, 1, 2, own - 1, own, own + 1):
        thickness(ch)

    for ch in edges:
        velocity(ch)
    copies += [
        pltpu.make_async_copy(
            edge_out.at[k, side],
            out.at[:, pl.ds(side * (columns - EDGE), EDGE), :],
            sems.at[k, side],
        )
        for k, out in enumerate((zonal_out, merid_out, thick_out))
        for side in range(2)
    ]
    for copy in copies[3:]:
        copy.start()

    take = block_features(spread, lat)
    blocks = lat // 2 + 2
    first, last = take(0), take(own)
    feat[0] = first
    feat[1, :, 0:128] = first[:, 128:256]
    feat[1, :, 128:256] = inner_feat[1, :, 128:256]
    feat[2, :, 0:128] = inner_feat[own - 1, :, 0:128]
    feat[2, :, 128:256] = last[:, 0:128]
    feat[3] = last

    south_end = jnp.where(oy == 0, 0.0, 1.0)
    north_end = jnp.where(oy == lat_count - 1, 0.0, 1.0)
    brow = lax.broadcasted_iota(jnp.int32, (8, 256), 0)
    quad = lax.broadcasted_iota(jnp.int32, (8, 256), 1) // 64 % 2
    low_1 = jnp.where(brow == 0, south_end, 1.0)
    high_1 = jnp.where(brow == blocks - 1 - 64, north_end, 1.0)
    low_2 = jnp.where((brow == 0) & (quad == 0), south_end, 1.0)
    high_2 = jnp.where((brow == blocks - 2 - 64) & (quad == 1), north_end, 1.0)

    def activate(total, bias, count, low, high):
        total = total + bias
        total = total * jnp.tanh(total) + total
        total = total.reshape(count, PITCH, 256)
        return jnp.concatenate(
            [total[:, 0:8] * low, total[:, 8:64], total[:, 64:72] * high, total[:, 72:]], axis=1
        )

    bias1 = b1[0:1, :]
    bias2 = b2[0:1, :]
    groups = inner_feat.shape[0]

    all_feat = jnp.concatenate([feat[0:2], inner_feat[2 : own - 1], feat[2:4]], axis=0)

    def first_step(t, count, n):
        left = all_feat[t : t + count].reshape(count * PITCH, 256)
        h = jnp.dot(left, w1[n], preferred_element_type=F32)
        h = activate(h, bias1, count, low_1, high_1)
        moved = pltpu.roll(h.reshape(count * PITCH, 256), count * PITCH - 1, 0)
        act[t : t + count, n] = h.astype(BF16)
        act_up[t : t + count, n] = moved.reshape(count, PITCH, 256).astype(BF16)

    for n in range(4):
        for t in range(0, groups, 6):
            first_step(t, min(6, groups - t), n)

    block_rows = columns // 2 + 1
    some = next(n for n in range(6, 0, -1) if block_rows % n == 0)
    flat = lambda ref: ref.reshape(4 * groups, PITCH, 256)
    first_act, first_up = flat(act), flat(act_up)

    def second_step(n, carry):
        at = n * some
        parts_of = [
            ref[pl.ds(at + shift, some)].reshape(some * PITCH, 256)
            for shift in range(2)
            for ref in (first_act, first_up)
        ]
        h = jnp.dot(jnp.concatenate(parts_of, axis=1), w2[...], preferred_element_type=F32)
        second[pl.ds(at, some)] = activate(h, bias2, some, low_2, high_2).astype(BF16)
        return carry

    for n in range(block_rows // some):
        second_step(n, 0)

    eights = columns // 16
    wide_left = [
        jnp.concatenate([second[8 * g + m] for g in range(eights)], axis=0) for m in range(8)
    ]
    total = jnp.dot(jnp.concatenate(wide_left, axis=1), w3[...], preferred_element_type=F32)
    pad = jnp.zeros((128 - PITCH, 128), F32)
    for g in range(eights):
        parts[128 * g : 128 * g + 128, :] = jnp.concatenate([total[PITCH * g : PITCH * (g + 1)], pad], axis=0).T
    end = jnp.dot(second[8 * eights], w3[0:256], preferred_element_type=F32)
    parts[128 * eights : 128 * eights + 16, :] = jnp.concatenate([end, pad], axis=0).T[0:16]

    for i in range(columns // 2):
        sums[8 * i : 8 * i + 8, :] = parts[16 * i : 16 * i + 8, :] + parts[16 * i + 24 : 16 * i + 32, :]
    jj = lax.broadcasted_iota(jnp.int32, (128, lat), 0)
    ll = lax.broadcasted_iota(jnp.int32, (128, lat), 1)
    out = jnp.zeros((columns, lat), F32)
    for k in range(4):
        x = sums[pl.ds(k, columns, stride=4), :]
        high = x.astype(BF16)
        rest = (x - high.astype(F32)).astype(BF16)
        put_at = jnp.where(ll == 2 * (jj - k // 2) + k % 2, 1.0, 0.0).astype(BF16)
        out = out + jnp.dot(high, put_at, preferred_element_type=F32)
        out = out + jnp.dot(rest, put_at, preferred_element_type=F32)
    visc_out[...] = jnp.exp(out)
    for copy in copies:
        copy.wait()


def swap(x, axis, parity, count, periodic):
    pairs = []
    for i in range(count):
        j = i + 1 if i % 2 == parity else i - 1
        if periodic or 0 <= j < count:
            pairs.append((i, j % count))
    return lax.ppermute(x, axis, pairs)


def local(
    nx,
    ny,
    zonal,
    merid,
    thick,
    land,
    visc,
    wind,
    gravity,
    conv_first,
    bias_first,
    conv_second,
    bias_second,
    conv_last,
):
    layers, columns, lat = zonal.shape
    big = pltpu.CompilerParams(vmem_limit_bytes=48 * 1024 * 1024)
    lon_rows = EDGE * FIELDS
    lat_a, lat_b = pl.pallas_call(
        pack_kernel,
        out_shape=[jax.ShapeDtypeStruct((columns, lat), BF16)] * 2,
        in_specs=[pl.BlockSpec(memory_space=pltpu.HBM)] * 6,
        out_specs=[VMEM] * 2,
        scratch_shapes=[pltpu.VMEM(a.shape, a.dtype) for a in (zonal, merid, thick, land, visc, wind)]
        + [pltpu.SemaphoreType.DMA] * 6,
        compiler_params=pltpu.CompilerParams(vmem_limit_bytes=62 * 1024 * 1024),
        name="pack",
    )(zonal, merid, thick, land, visc, wind)
    lat_a = swap(lat_a, "oy", 0, ny, False)
    lat_b = swap(lat_b, "oy", 1, ny, False)
    w1, w2, w3, b1, b2, grav = pl.pallas_call(
        weight_kernel,
        out_shape=[
            jax.ShapeDtypeStruct((4, 256, 256), BF16),
            jax.ShapeDtypeStruct((1024, 256), BF16),
            jax.ShapeDtypeStruct((2048, 128), BF16),
            jax.ShapeDtypeStruct((8, 256), F32),
            jax.ShapeDtypeStruct((8, 256), F32),
            jax.ShapeDtypeStruct((layers, 8, 2 * lat), F32),
        ],
        in_specs=[VMEM] * 6,
        out_specs=[VMEM] * 6,
        compiler_params=big,
        name="weights",
    )(conv_first, conv_second, conv_last, bias_first[None], bias_second[None], gravity[None])
    flow = jax.ShapeDtypeStruct((layers, columns, lat), F32)
    flat = jax.ShapeDtypeStruct((columns, lat), F32)
    outer = columns + 4 * EDGE
    inputs = (zonal, merid, thick, land, visc, wind)
    own = pl.pallas_call(
        functools.partial(own_kernel, ny),
        out_shape=[flow] * 3 + [flat] * 3,
        in_specs=[VMEM] * 7,
        out_specs=[VMEM] * 6,
        scratch_shapes=[
            pltpu.VMEM((FIELDS, outer, lat), F32),
            pltpu.VMEM((layers, outer, lat), F32),
            pltpu.VMEM((layers, outer, lat), F32),
        ],
        compiler_params=big,
        cost_estimate=pl.CostEstimate(flops=20_000_000, bytes_accessed=4_000_000, transcendentals=0),
        name="own",
    )(*inputs, grav)
    lon_a, lon_b = pl.pallas_call(
        lon_kernel,
        out_shape=[jax.ShapeDtypeStruct((lon_rows + 32, lat), BF16)] * 2,
        in_specs=[VMEM] * 8 + [pl.BlockSpec(memory_space=pl.ANY)],
        out_specs=[VMEM] * 2,
        compiler_params=big,
        name="lon",
    )(*inputs, lat_a, lat_b, own[3])
    lon_a = swap(lon_a, "ox", 0, nx, True)
    lon_b = swap(lon_b, "ox", 1, nx, True)
    wide = 2 * lat
    groups = columns // 8 + 1
    work = [
        pltpu.VMEM((FIELDS, outer, wide), F32),
        pltpu.VMEM((layers, outer, wide), F32),
        pltpu.VMEM((layers, outer, wide), F32),
        pltpu.VMEM((columns + 2 * EDGE, 16, wide), F32),
    ]
    zonal_mid, merid_mid, thick_mid, feat, edge_ext = pl.pallas_call(
        functools.partial(inner_kernel, ny),
        out_shape=[
            flow,
            flow,
            flow,
            jax.ShapeDtypeStruct((groups, PITCH, 256), BF16),
            jax.ShapeDtypeStruct((FIELDS, 48, wide), F32),
        ],
        in_specs=[VMEM] * 15,
        out_specs=[VMEM] * 5,
        scratch_shapes=[
            pltpu.VMEM((7, outer, lat), F32),
            pltpu.VMEM((outer, lat), F32),
            pltpu.VMEM((outer, lat), F32),
            pltpu.VMEM((columns + 2 * EDGE, 16, wide), F32),
        ],
        compiler_params=big,
        cost_estimate=pl.CostEstimate(flops=40_000_000, bytes_accessed=8_000_000, transcendentals=0),
        name="inner",
    )(*inputs, grav, lat_a, lat_b, *own)
    hbm = pl.BlockSpec(memory_space=pltpu.HBM)
    return pl.pallas_call(
        functools.partial(main_kernel, ny),
        out_shape=[flow] * 3 + [jax.ShapeDtypeStruct((columns, lat), F32)],
        in_specs=[VMEM] * 13,
        out_specs=[hbm] * 3 + [VMEM],
        scratch_shapes=work
        + [
            pltpu.VMEM((4, PITCH, 256), BF16),
            pltpu.VMEM((groups, 4, PITCH, 256), BF16),
            pltpu.VMEM((groups, 4, PITCH, 256), BF16),
            pltpu.VMEM((columns // 2 + 1, PITCH, 256), BF16),
            pltpu.VMEM((8 * columns + 16, 128), F32),
            pltpu.VMEM((4 * columns, 128), F32),
            pltpu.VMEM((3, 2, layers, EDGE, lat), F32),
            pltpu.SemaphoreType.DMA((3, 3)),
        ],
        compiler_params=big,
        name="step",
    )(
        zonal_mid,
        merid_mid,
        thick_mid,
        grav,
        lon_a,
        lon_b,
        feat,
        edge_ext,
        w1,
        w2,
        w3,
        b1,
        b2,
    )


def solution(mesh):
    in_specs = (
        P(None, "ox", "oy"),
        P(None, "ox", "oy"),
        P(None, "ox", "oy"),
        P("ox", "oy"),
        P("ox", "oy"),
        P(None, "ox", "oy"),
        P(),
        P(),
        P(),
        P(),
        P(),
        P(),
    )
    out_specs = (P(None, "ox", "oy"), P(None, "ox", "oy"), P(None, "ox", "oy"), P("ox", "oy"))
    body = functools.partial(local, mesh.shape["ox"], mesh.shape["oy"])
    return jax.shard_map(body, mesh=mesh, in_specs=in_specs, out_specs=out_specs, check_vma=False)
```

```python
import functools

import jax
import jax.numpy as jnp
from jax import lax
from jax.experimental import pallas as pl
from jax.experimental.pallas import tpu as pltpu
from jax.sharding import PartitionSpec as P

TIME_STEP = 0.05
REST_DEPTH = 1.4
DRAG_RATE = 0.5

F32 = jnp.float32
BF16 = jnp.bfloat16
EDGE = 8
FIELDS = 16
PITCH = 80
VMEM = pl.BlockSpec(memory_space=pltpu.VMEM)


def slot(f):
    return 4 * (f % 4) + f // 4


def own_fields(zonal, merid, thick, land, visc, wind, rows):
    sea = land[rows, :].astype(F32)
    layers = zonal.shape[0]
    maps = [zonal[l, rows, :] * sea for l in range(layers)]
    maps += [merid[l, rows, :] * sea for l in range(layers)]
    maps += [thick[l, rows, :] - REST_DEPTH for l in range(layers)]
    return maps + [sea, visc[rows, :], wind[0, rows, :], wind[1, rows, :]]


def pack_kernel(*refs):
    sources, (lat_a, lat_b), held, sems = refs[:6], refs[6:8], refs[8:14], refs[14:]
    copies = [pltpu.make_async_copy(*each) for each in zip(sources, held, sems)]
    for copy in copies:
        copy.start()
    for copy in copies:
        copy.wait()
    zonal, merid, thick, land, visc, wind = held
    columns, lat = land.shape
    even_y = lax.rem(lax.axis_index("oy"), 2) == 0
    lane = lax.broadcasted_iota(jnp.int32, (16, lat), 1) // EDGE
    for c in range(0, columns, 16):
        low = jnp.zeros((16, lat), F32)
        high = jnp.zeros((16, lat), F32)
        for f, field in enumerate(own_fields(zonal, merid, thick, land, visc, wind, slice(c, c + 16))):
            here = lane == slot(f)
            low = jnp.where(here, pltpu.roll(field, EDGE * slot(f) % lat, 1), low)
            high = jnp.where(here, pltpu.roll(field, (EDGE * slot(f) + EDGE) % lat, 1), high)
        lat_a[c : c + 16, :] = jnp.where(even_y, high, low).astype(BF16)
        lat_b[c : c + 16, :] = jnp.where(even_y, low, high).astype(BF16)


def lon_kernel(zonal, merid, thick, land, visc, wind, got_a, got_b, after, lon_a, lon_b):
    del after
    columns = got_a.shape[0]
    even_x = lax.rem(lax.axis_index("ox"), 2) == 0
    size = EDGE * FIELDS
    maps_low = own_fields(zonal, merid, thick, land, visc, wind, slice(0, EDGE))
    maps_high = own_fields(zonal, merid, thick, land, visc, wind, slice(columns - EDGE, columns))
    for f in range(0, FIELDS, 2):
        low = jnp.concatenate(maps_low[f : f + 2], axis=0)
        high = jnp.concatenate(maps_high[f : f + 2], axis=0)
        lon_a[EDGE * f : EDGE * f + 16, :] = jnp.where(even_x, high, low).astype(BF16)
        lon_b[EDGE * f : EDGE * f + 16, :] = jnp.where(even_x, low, high).astype(BF16)
    for n, got in enumerate((got_a, got_b)):
        low = got[0:16, :]
        high = got[columns - 16 : columns, :]
        lon_a[size + 16 * n : size + 16 * n + 16, :] = jnp.where(even_x, high, low)
        lon_b[size + 16 * n : size + 16 * n + 16, :] = jnp.where(even_x, low, high)


def weight_kernel(first, second, last, bias_first, bias_second, gravity, w1, w2, w3, b1, b2, grav):
    hidden = second.shape[2]
    zero = jnp.zeros((hidden, hidden), F32)
    turned = [[second[a, b].astype(F32).T * 0.5 for b in range(3)] for a in range(3)]
    tap = lambda a, b: turned[a][b] if 0 <= a < 3 and 0 <= b < 3 else zero
    for px in range(4):
        for py in range(4):
            ex, ey, a, b = px % 2, py % 2, px // 2, py // 2
            row = ((2 * a + b) * 4 + 2 * ex + ey) * hidden
            for dx in range(2):
                w2[row : row + hidden, 128 * dx : 128 * dx + 128] = jnp.concatenate(
                    [tap(px - dx, py), tap(px - dx, py - 1)], axis=1
                ).astype(BF16)
    feats = first.shape[3]
    spot = lax.broadcasted_iota(jnp.int32, (256, feats), 0)
    chan = lax.broadcasted_iota(jnp.int32, (256, feats), 1)
    total = jnp.zeros((256, hidden), F32)
    ddx, ddy = spot // 128, (spot // 64) % 2
    for a in range(3):
        for b in range(3):
            want = ((ddx + a) * 4 + ddy + b) * feats + chan
            place = jnp.where(spot % 64 == want, 0.5, 0.0).astype(BF16)
            total = total + lax.dot_general(
                place, first[a, b], (((1,), (1,)), ((), ())), preferred_element_type=F32
            )
    base = jnp.concatenate(
        [
            jnp.concatenate([total[0:64], total[64:128]], axis=1),
            jnp.concatenate([total[128:192], total[192:256]], axis=1),
        ],
        axis=1,
    )
    for s in range(4):
        off = 80 + 32 * s
        w1[s] = jnp.concatenate(
            [jnp.zeros((off, 256), F32), base, jnp.zeros((192 - off, 256), F32)], axis=0
        ).astype(BF16)
    row = lax.broadcasted_iota(jnp.int32, (16, 128), 0)
    blank = jnp.zeros((1, hidden), F32)
    piece = lambda a, b: last[a, b].astype(F32) if 0 <= a < 3 and 0 <= b < 3 else blank
    for ex in range(2):
        tile = jnp.zeros((16, 128), F32)
        for k in range(16):
            a, dx, b, dy = k // 8, (k // 4) % 2, (k // 2) % 2, k % 2
            p, q = 2 * a + ex - dx, 2 * b - dy
            line = jnp.concatenate([piece(p, q), piece(p, q + 1)], axis=1)
            tile = jnp.where(row == k, jnp.broadcast_to(line, (16, 128)), tile)
        turned_tile = jnp.concatenate([tile] * 8, axis=0).T
        lane = lax.broadcasted_iota(jnp.int32, (128, 128), 1) // 16
        for m in range(8):
            start = 256 * m + 128 * ex
            w3[start : start + 128, :] = jnp.where(lane == m, turned_tile, 0.0).astype(BF16)
    for bias, out in ((bias_first, b1), (bias_second, b2)):
        half = bias[...] * 0.5
        out[...] = jnp.broadcast_to(jnp.concatenate([half] * 4, axis=1), (8, 256))
    for l in range(grav.shape[0]):
        grav[l] = jnp.broadcast_to(gravity[0:1, l : l + 1], grav.shape[1:])


def far_tile(n_rows, s_rows, f):
    lat = n_rows.shape[1]
    lane = lax.broadcasted_iota(jnp.int32, n_rows.shape, 1)
    up = pltpu.roll(n_rows, (lat - EDGE * slot(f)) % lat, 1)
    down = pltpu.roll(s_rows, (2 * lat - EDGE - EDGE * slot(f)) % lat, 1)
    return jnp.where(lane < EDGE, up, jnp.where(lane >= lat - EDGE, down, 0.0))


def dynamics(layers, wide, lat, lat_count, ext, nxt, prs, grav, store, emit):
    oy = lax.axis_index("oy")
    sea_id, visc_id, wind_id = 3 * layers, 3 * layers + 1, 3 * layers + 2
    place = lax.broadcasted_iota(jnp.int32, (EDGE, wide), 1)
    if wide > lat:
        place = jnp.where(place < lat + lat // 2, place, place - wide)
    coriolis = 0.3 + 1.4 * ((oy * lat + place).astype(F32) + 0.5) / (lat_count * lat)

    def up(x):
        return pltpu.roll(x, wide - 1, 1)

    def down(x):
        return pltpu.roll(x, 1, 1)

    def rows_of(ch):
        r = EDGE + EDGE * ch
        return slice(r, r + 8), slice(r + 1, r + 9), slice(r - 1, r + 7)

    def thickness(ch):
        here, plus, minus = rows_of(ch)
        sea = ext[sea_id, here, :]
        odd = []
        for l in range(layers):
            h = ext[2 * layers + l, here, :]
            flux_e = ext[l, plus, :] * ext[2 * layers + l, plus, :]
            flux_w = ext[l, minus, :] * ext[2 * layers + l, minus, :]
            flux_y = ext[layers + l, here, :] * h
            diverge = (flux_e - flux_w) * 0.5 + (up(flux_y) - down(flux_y)) * 0.5
            h = h - TIME_STEP * sea * diverge
            nxt[l, here, :] = h
            odd.append(h - REST_DEPTH)
        for l in reversed(range(layers - 1)):
            odd[l] = odd[l] + odd[l + 1]
        total = jnp.zeros_like(sea)
        for l in range(layers):
            total = total + grav[l, :, 0:wide] * odd[l]
            prs[l, here, :] = total

    def velocity(ch):
        here, plus, minus = rows_of(ch)
        sea = ext[sea_id, here, :]
        v = ext[visc_id, here, :]
        mix = [
            0.5 * (v + ext[visc_id, plus, :]),
            0.5 * (v + ext[visc_id, minus, :]),
            0.5 * (v + up(v)),
            0.5 * (v + down(v)),
        ]

        def lap(f, q):
            near = (ext[f, plus, :], ext[f, minus, :], up(q), down(q))
            total = mix[0] * (near[0] - q)
            for side in range(1, 4):
                total = total + mix[side] * (near[side] - q)
            return total

        heavy = jnp.zeros_like(sea)
        moving = jnp.zeros_like(sea)
        for l in range(layers):
            zm = ext[l, here, :]
            vm = ext[layers + l, here, :]
            p = prs[l, here, :]
            h = nxt[l, here, :]
            grad_x = (prs[l, plus, :] - prs[l, minus, :]) * 0.5
            grad_y = (up(p) - down(p)) * 0.5
            push_x = coriolis * vm - grad_x + lap(l, zm)
            push_y = -coriolis * zm - grad_y + lap(layers + l, vm)
            if l == 0:
                push_x = push_x + ext[wind_id, here, :] / h
                push_y = push_y + ext[wind_id + 1, here, :] / h
            if l == layers - 1:
                push_x = push_x - DRAG_RATE * zm
                push_y = push_y - DRAG_RATE * vm
            zn = sea * (zm + TIME_STEP * push_x)
            vn = sea * (vm + TIME_STEP * push_y)
            store(ch, l, zn[:, 0:lat], vn[:, 0:lat], h[:, 0:lat])
            heavy = heavy + h
            moving = moving + h * (zn * zn + vn * vn)
            if l == 0:
                maps = [zn, vn, sea * (h - REST_DEPTH)]
        maps.append(sea * (0.5 * moving / heavy))
        emit(ch, maps)

    return thickness, velocity


def block_features(spread, lat):
    wide = 2 * lat
    block = lax.broadcasted_iota(jnp.int32, (PITCH, wide), 0)
    source = lax.broadcasted_iota(jnp.int32, (PITCH, wide), 1)
    chooser = jnp.where(
        (block < lat // 2 + 2) & (source == lax.rem(wide - 3 + 2 * block, wide)), 1.0, 0.0
    ).astype(BF16)

    def take(t):
        got = spread[8 * t : 8 * t + 16].reshape(256, wide).astype(BF16)
        return lax.dot_general(
            chooser, got, (((1,), (1,)), ((), ())), preferred_element_type=F32
        ).astype(BF16)

    return take


def scatter(spread, row, maps, wide):
    for f, m in enumerate(maps):
        for dy in range(4):
            spread[row : row + m.shape[0], 4 * dy + f, :] = pltpu.roll(m, (wide - dy) % wide, 1) if dy else m


def own_kernel(
    lat_count,
    zonal,
    merid,
    thick,
    land,
    visc,
    wind,
    grav,
    zonal_own,
    merid_own,
    thick_own,
    energy_own,
    low_out,
    high_out,
    ext,
    nxt,
    prs,
):
    layers, columns, lat = zonal.shape
    base = 2 * EDGE
    group = lax.broadcasted_iota(jnp.int32, (EDGE, lat), 1) // EDGE
    for c in range(0, columns, EDGE):
        rows = slice(c, c + EDGE)
        low = jnp.zeros((EDGE, lat), F32)
        high = jnp.zeros((EDGE, lat), F32)
        for f, field in enumerate(own_fields(zonal, merid, thick, land, visc, wind, rows)):
            here = group == slot(f)
            low = jnp.where(here, pltpu.roll(field, EDGE * slot(f) % lat, 1), low)
            high = jnp.where(here, pltpu.roll(field, (EDGE * slot(f) + EDGE) % lat, 1), high)
            if 2 * layers <= f < 3 * layers:
                field = thick[f - 2 * layers, rows, :]
            ext[f, base + c : base + c + EDGE, :] = field
        low_out[rows, :] = low
        high_out[rows, :] = high

    def store(ch, l, zn, vn, h):
        row = EDGE * ch - EDGE
        zonal_own[l, row : row + 8, :] = zn
        merid_own[l, row : row + 8, :] = vn
        thick_own[l, row : row + 8, :] = h

    def emit(ch, maps):
        row = EDGE * ch - EDGE
        energy_own[row : row + 8, :] = maps[3]

    thickness, velocity = dynamics(layers, lat, lat, lat_count, ext, nxt, prs, grav, store, emit)
    own = columns // EDGE
    for ch in range(1, own + 1):
        thickness(ch)
    for ch in range(2, own):
        velocity(ch)


def inner_kernel(
    lat_count,
    zonal,
    merid,
    thick,
    land,
    visc,
    wind,
    grav,
    lat_a,
    lat_b,
    zonal_own,
    merid_own,
    thick_own,
    energy_own,
    low_own,
    high_own,
    zonal_out,
    merid_out,
    thick_out,
    feat,
    edge_ext,
    strip,
    nxt,
    prs,
    spread,
):
    layers, columns, lat = zonal.shape
    oy = lax.axis_index("oy")
    even_y = lax.rem(oy, 2) == 0
    base = 2 * EDGE
    wide = 2 * lat
    own = columns // EDGE
    part = lat // layers
    lane = lax.broadcasted_iota(jnp.int32, (EDGE, lat), 1)
    layer = lane // part
    spot = lane % part

    def turn(x, shift):
        return pltpu.roll(x, shift % lat, 1) if shift % lat else x

    edge_rows = {0: 0, 8: 8, 16: 16, columns - 24: 24, columns - 16: 32, columns - 8: 40}
    for c in range(0, columns, 16):
        got_a = lat_a[c : c + 16, :].astype(F32)
        got_b = lat_b[c : c + 16, :].astype(F32)
        n_both = jnp.where(even_y, got_a, got_b)
        s_both = jnp.where(even_y, got_b, got_a)
        for h in range(0, 16, EDGE):
            rows = slice(c + h, c + h + EDGE)
            north, south = n_both[h : h + EDGE], s_both[h : h + EDGE]
            low, high = low_own[rows, :], high_own[rows, :]
            four = []
            for g in range(4):
                tile = jnp.where(spot < 24, turn(high, 16 - 8 * g), turn(north, 24 - 8 * g))
                tile = jnp.where(spot < 16, turn(low, 8 - 8 * g), tile)
                four.append(jnp.where(spot < 8, turn(south, -8 * g), tile))
            four[2] = four[2] + REST_DEPTH
            other = four.pop()
            sea, v = other, turn(other, -part)
            for l in range(1, layers):
                sea = jnp.where(layer == l, turn(other, part * l), sea)
                v = jnp.where(layer == l, turn(other, part * (l - 1)), v)
            four += [sea, v, turn(other, -2 * part), turn(other, -3 * part)]
            row = base + c + h
            for n, tile in enumerate(four):
                strip[n, row : row + EDGE, :] = tile
            edge = edge_rows.get(c + h)
            if edge is not None:
                maps = own_fields(zonal, merid, thick, land, visc, wind, rows)
                for f in range(FIELDS):
                    lift = REST_DEPTH if 2 * layers <= f < 3 * layers else 0.0
                    first = thick[f - 2 * layers, rows, :] if lift else maps[f]
                    edge_ext[f, edge : edge + EDGE, 0:lat] = first
                    edge_ext[f, edge : edge + EDGE, lat:wide] = far_tile(north, south, f) + lift

    def lanes(rows):
        at = lax.broadcasted_iota(jnp.int32, (rows, lat), 1)
        return at, at // part, at % part

    up = lambda x: turn(x, -1)
    down = lambda x: turn(x, 1)

    some = columns // 1
    lane, layer, spot = lanes(some)
    pull = jnp.broadcast_to(grav[0, 0:1, 0:lat], (some, lat))
    for l in range(1, layers):
        pull = jnp.where(layer == l, jnp.broadcast_to(grav[l, 0:1, 0:lat], (some, lat)), pull)
    for r in range(base, base + columns, some):
        here, plus, minus = slice(r, r + some), slice(r + 1, r + some + 1), slice(r - 1, r + some - 1)
        h = strip[2, here, :]
        flux_y = strip[1, here, :] * h
        flux_e = strip[0, plus, :] * strip[2, plus, :]
        flux_w = strip[0, minus, :] * strip[2, minus, :]
        diverge = (flux_e - flux_w) * 0.5 + (up(flux_y) - down(flux_y)) * 0.5
        h = h - TIME_STEP * strip[3, here, :] * diverge
        nxt[here, :] = h
        total = h - REST_DEPTH
        total = total + jnp.where(layer < 3, turn(total, -part), 0.0)
        total = total + jnp.where(layer < 2, turn(total, -2 * part), 0.0)
        total = total * pull
        total = total + jnp.where(layer >= 1, turn(total, part), 0.0)
        prs[here, :] = total + jnp.where(layer >= 2, turn(total, 2 * part), 0.0)

    def over_layers(x):
        x = x + turn(x, part)
        return x + turn(x, 2 * part)

    def patch(tile, result, l):
        tile = jnp.where(lane < 2, turn(result, -EDGE - part * l), tile)
        return jnp.where(lane >= lat - 2, turn(result, lat - 24 - part * l), tile)

    some = (columns - 2 * EDGE) // 1
    lane, layer, spot = lanes(some)
    place = jnp.where(spot < 16, spot - EDGE, lat - EDGE + spot - 16)
    coriolis = 0.3 + 1.4 * ((oy * lat + place).astype(F32) + 0.5) / (lat_count * lat)
    drag = jnp.where(layer == layers - 1, DRAG_RATE, 0.0)
    for r in range(base + EDGE, base + columns - EDGE, some):
        here, plus, minus = slice(r, r + some), slice(r + 1, r + some + 1), slice(r - 1, r + some - 1)
        row = slice(r - base, r - base + some)
        v = strip[4, here, :]
        mix = [
            0.5 * (v + strip[4, plus, :]),
            0.5 * (v + strip[4, minus, :]),
            0.5 * (v + up(v)),
            0.5 * (v + down(v)),
        ]

        def lap(n, q):
            near = (strip[n, plus, :], strip[n, minus, :], up(q), down(q))
            total = mix[0] * (near[0] - q)
            for side in range(1, 4):
                total = total + mix[side] * (near[side] - q)
            return total

        sea = strip[3, here, :]
        zm, vm = strip[0, here, :], strip[1, here, :]
        h, p = nxt[here, :], prs[here, :]
        grad_x = (prs[plus, :] - prs[minus, :]) * 0.5
        grad_y = (up(p) - down(p)) * 0.5
        wind_x = jnp.where(layer == 0, strip[5, here, :] / h, 0.0)
        wind_y = jnp.where(layer == 0, strip[6, here, :] / h, 0.0)
        zn = sea * (zm + TIME_STEP * (coriolis * vm - grad_x + lap(0, zm) + wind_x - drag * zm))
        vn = sea * (vm + TIME_STEP * (-coriolis * zm - grad_y + lap(1, vm) + wind_y - drag * vm))
        energy = sea * (0.5 * over_layers(h * (zn * zn + vn * vn)) / over_layers(h))
        for l in range(layers):
            for source, result, out in (
                (zonal_own, zn, zonal_out),
                (merid_own, vn, merid_out),
                (thick_own, h, thick_out),
            ):
                out[l, row, :] = patch(source[l, row, :], result, l)
        own_sea = land[row, :].astype(F32)
        maps = []
        for tile, result in (
            (zonal_own[0, row, :], zn),
            (merid_own[0, row, :], vn),
            (own_sea * (thick_own[0, row, :] - REST_DEPTH), sea * (h - REST_DEPTH)),
            (energy_own[row, :], energy),
        ):
            far = jnp.where(lane < 3, turn(result, -24), jnp.where(lane >= lat - 3, turn(result, -8), 0.0))
            maps.append(jnp.concatenate([patch(tile, result, 0), far], axis=1))
        scatter(spread, r - EDGE, maps, wide)

    take = block_features(spread, lat)
    for t in range(2, own, 2):
        g = take(t)
        feat[t] = g
        feat[t + 1, :, 0:128] = g[:, 128:256]
        feat[t - 1, :, 128:256] = g[:, 0:128]


def main_kernel(
    lat_count,
    zonal_in,
    merid_in,
    thick_in,
    grav,
    lon_a,
    lon_b,
    inner_feat,
    edge_ext,
    w1,
    w2,
    w3,
    b1,
    b2,
    zonal_out,
    merid_out,
    thick_out,
    visc_out,
    ext,
    nxt,
    prs,
    spread,
    feat,
    act,
    act_up,
    second,
    parts,
    sums,
    edge_out,
    sems,
):
    columns, lat = visc_out.shape
    layers = grav.shape[0]
    oy = lax.axis_index("oy")
    even_y = lax.rem(oy, 2) == 0
    even_x = lax.rem(lax.axis_index("ox"), 2) == 0
    base = 2 * EDGE
    wide = 2 * lat
    own = columns // EDGE

    inside = pl.ds(EDGE, columns - 2 * EDGE)
    copies = [
        pltpu.make_async_copy(mid.at[:, inside, :], out.at[:, inside, :], sems.at[k, 2])
        for k, (mid, out) in enumerate(((zonal_in, zonal_out), (merid_in, merid_out), (thick_in, thick_out)))
    ]
    for copy in copies:
        copy.start()

    west = jnp.where(even_x, lon_b[...], lon_a[...])
    east = jnp.where(even_x, lon_a[...], lon_b[...])
    size = EDGE * FIELDS
    for side, slot, row in ((west, slice(8, 16), base - EDGE), (east, slice(0, 8), base + columns)):
        from_a = side[size : size + 16].astype(F32)[slot]
        from_b = side[size + 16 : size + 32].astype(F32)[slot]
        north = jnp.where(even_y, from_a, from_b)
        south = jnp.where(even_y, from_b, from_a)
        near = side[:size].astype(F32)
        for f in range(FIELDS):
            lift = REST_DEPTH if 2 * layers <= f < 3 * layers else 0.0
            ext[f, row : row + EDGE, 0:lat] = near[EDGE * f : EDGE * f + EDGE] + lift
            ext[f, row : row + EDGE, lat:wide] = far_tile(north, south, f) + lift
    for f in range(FIELDS):
        ext[f, base : base + 24, :] = edge_ext[f, 0:24, :]
        ext[f, base + columns - 24 : base + columns, :] = edge_ext[f, 24:48, :]

    def store(ch, l, zn, vn, h):
        if ch in (1, own):
            side = 0 if ch == 1 else 1
            for k, tile in enumerate((zn, vn, h)):
                edge_out[k, side, l] = tile

    place = lax.broadcasted_iota(jnp.int32, (EDGE, wide), 1)
    in_lat = (place < lat + 3) | (place >= wide - 3)

    def emit(ch, maps):
        column = lax.broadcasted_iota(jnp.int32, (EDGE, wide), 0) + (EDGE + EDGE * ch - base)
        keep = in_lat & (column >= -3) & (column < columns + 3)
        scatter(spread, EDGE * ch, [jnp.where(keep, m, 0.0) for m in maps], wide)

    thickness, velocity = dynamics(layers, wide, lat, lat_count, ext, nxt, prs, grav, store, emit)
    edges = (0, 1, own, own + 1)
    for ch in (0, 1, 2, own - 1, own, own + 1):
        thickness(ch)

    for ch in edges:
        velocity(ch)
    copies += [
        pltpu.make_async_copy(
            edge_out.at[k, side],
            out.at[:, pl.ds(side * (columns - EDGE), EDGE), :],
            sems.at[k, side],
        )
        for k, out in enumerate((zonal_out, merid_out, thick_out))
        for side in range(2)
    ]
    for copy in copies[3:]:
        copy.start()

    take = block_features(spread, lat)
    blocks = lat // 2 + 2
    first, last = take(0), take(own)
    feat[0] = first
    feat[1, :, 0:128] = first[:, 128:256]
    feat[1, :, 128:256] = inner_feat[1, :, 128:256]
    feat[2, :, 0:128] = inner_feat[own - 1, :, 0:128]
    feat[2, :, 128:256] = last[:, 0:128]
    feat[3] = last

    south_end = jnp.where(oy == 0, 0.0, 1.0)
    north_end = jnp.where(oy == lat_count - 1, 0.0, 1.0)
    brow = lax.broadcasted_iota(jnp.int32, (8, 256), 0)
    quad = lax.broadcasted_iota(jnp.int32, (8, 256), 1) // 64 % 2
    low_1 = jnp.where(brow == 0, south_end, 1.0)
    high_1 = jnp.where(brow == blocks - 1 - 64, north_end, 1.0)
    low_2 = jnp.where((brow == 0) & (quad == 0), south_end, 1.0)
    high_2 = jnp.where((brow == blocks - 2 - 64) & (quad == 1), north_end, 1.0)

    def activate(total, bias, count, low, high):
        total = total + bias
        total = total * jnp.tanh(total) + total
        total = total.reshape(count, PITCH, 256)
        return jnp.concatenate(
            [total[:, 0:8] * low, total[:, 8:64], total[:, 64:72] * high, total[:, 72:]], axis=1
        )

    bias1 = b1[0:1, :]
    bias2 = b2[0:1, :]
    groups = inner_feat.shape[0]

    all_feat = jnp.concatenate([feat[0:2], inner_feat[2 : own - 1], feat[2:4]], axis=0)

    def first_step(t, count, n):
        left = all_feat[t : t + count].reshape(count * PITCH, 256)
        h = jnp.dot(left, w1[n], preferred_element_type=F32)
        h = activate(h, bias1, count, low_1, high_1)
        moved = pltpu.roll(h.reshape(count * PITCH, 256), count * PITCH - 1, 0)
        act[t : t + count, n] = h.astype(BF16)
        act_up[t : t + count, n] = moved.reshape(count, PITCH, 256).astype(BF16)

    for n in range(4):
        for t in range(0, groups, 6):
            first_step(t, min(6, groups - t), n)

    block_rows = columns // 2 + 1
    some = next(n for n in range(6, 0, -1) if block_rows % n == 0)
    flat = lambda ref: ref.reshape(4 * groups, PITCH, 256)
    first_act, first_up = flat(act), flat(act_up)

    def second_step(n, carry):
        at = n * some
        parts_of = [
            ref[pl.ds(at + shift, some)].reshape(some * PITCH, 256)
            for shift in range(2)
            for ref in (first_act, first_up)
        ]
        h = jnp.dot(jnp.concatenate(parts_of, axis=1), w2[...], preferred_element_type=F32)
        second[pl.ds(at, some)] = activate(h, bias2, some, low_2, high_2).astype(BF16)
        return carry

    for n in range(block_rows // some):
        second_step(n, 0)

    eights = columns // 16
    wide_left = [
        jnp.concatenate([second[8 * g + m] for g in range(eights)], axis=0) for m in range(8)
    ]
    total = jnp.dot(jnp.concatenate(wide_left, axis=1), w3[...], preferred_element_type=F32)
    pad = jnp.zeros((128 - PITCH, 128), F32)
    for g in range(eights):
        parts[128 * g : 128 * g + 128, :] = jnp.concatenate([total[PITCH * g : PITCH * (g + 1)], pad], axis=0).T
    end = jnp.dot(second[8 * eights], w3[0:256], preferred_element_type=F32)
    parts[128 * eights : 128 * eights + 16, :] = jnp.concatenate([end, pad], axis=0).T[0:16]

    for i in range(columns // 2):
        sums[8 * i : 8 * i + 8, :] = parts[16 * i : 16 * i + 8, :] + parts[16 * i + 24 : 16 * i + 32, :]
    jj = lax.broadcasted_iota(jnp.int32, (128, lat), 0)
    ll = lax.broadcasted_iota(jnp.int32, (128, lat), 1)
    out = jnp.zeros((columns, lat), F32)
    for k in range(4):
        x = sums[pl.ds(k, columns, stride=4), :]
        high = x.astype(BF16)
        rest = (x - high.astype(F32)).astype(BF16)
        put_at = jnp.where(ll == 2 * (jj - k // 2) + k % 2, 1.0, 0.0).astype(BF16)
        out = out + jnp.dot(high, put_at, preferred_element_type=F32)
        out = out + jnp.dot(rest, put_at, preferred_element_type=F32)
    visc_out[...] = jnp.exp(out)
    for copy in copies:
        copy.wait()


def swap(x, axis, parity, count, periodic):
    pairs = []
    for i in range(count):
        j = i + 1 if i % 2 == parity else i - 1
        if periodic or 0 <= j < count:
            pairs.append((i, j % count))
    return lax.ppermute(x, axis, pairs)


def local(
    nx,
    ny,
    zonal,
    merid,
    thick,
    land,
    visc,
    wind,
    gravity,
    conv_first,
    bias_first,
    conv_second,
    bias_second,
    conv_last,
):
    layers, columns, lat = zonal.shape
    big = pltpu.CompilerParams(vmem_limit_bytes=48 * 1024 * 1024)
    lon_rows = EDGE * FIELDS
    lat_a, lat_b = pl.pallas_call(
        pack_kernel,
        out_shape=[pltpu.VMEM((columns, lat), BF16)] * 2,
        in_specs=[pl.BlockSpec(memory_space=pltpu.HBM)] * 6,
        out_specs=[VMEM] * 2,
        scratch_shapes=[pltpu.VMEM(a.shape, a.dtype) for a in (zonal, merid, thick, land, visc, wind)]
        + [pltpu.SemaphoreType.DMA] * 6,
        compiler_params=pltpu.CompilerParams(vmem_limit_bytes=62 * 1024 * 1024),
        name="pack",
    )(zonal, merid, thick, land, visc, wind)
    lat_a = swap(lat_a, "oy", 0, ny, False)
    lat_b = swap(lat_b, "oy", 1, ny, False)
    w1, w2, w3, b1, b2, grav = pl.pallas_call(
        weight_kernel,
        out_shape=[
            jax.ShapeDtypeStruct((4, 256, 256), BF16),
            jax.ShapeDtypeStruct((1024, 256), BF16),
            jax.ShapeDtypeStruct((2048, 128), BF16),
            jax.ShapeDtypeStruct((8, 256), F32),
            jax.ShapeDtypeStruct((8, 256), F32),
            jax.ShapeDtypeStruct((layers, 8, 2 * lat), F32),
        ],
        in_specs=[VMEM] * 6,
        out_specs=[VMEM] * 6,
        compiler_params=big,
        name="weights",
    )(conv_first, conv_second, conv_last, bias_first[None], bias_second[None], gravity[None])
    flow = jax.ShapeDtypeStruct((layers, columns, lat), F32)
    flat = jax.ShapeDtypeStruct((columns, lat), F32)
    outer = columns + 4 * EDGE
    inputs = (zonal, merid, thick, land, visc, wind)
    own = pl.pallas_call(
        functools.partial(own_kernel, ny),
        out_shape=[flow] * 3 + [flat] * 3,
        in_specs=[VMEM] * 7,
        out_specs=[VMEM] * 6,
        scratch_shapes=[
            pltpu.VMEM((FIELDS, outer, lat), F32),
            pltpu.VMEM((layers, outer, lat), F32),
            pltpu.VMEM((layers, outer, lat), F32),
        ],
        compiler_params=big,
        cost_estimate=pl.CostEstimate(flops=20_000_000, bytes_accessed=4_000_000, transcendentals=0),
        name="own",
    )(*inputs, grav)
    lon_a, lon_b = pl.pallas_call(
        lon_kernel,
        out_shape=[jax.ShapeDtypeStruct((lon_rows + 32, lat), BF16)] * 2,
        in_specs=[VMEM] * 8 + [pl.BlockSpec(memory_space=pl.ANY)],
        out_specs=[VMEM] * 2,
        compiler_params=big,
        name="lon",
    )(*inputs, lat_a, lat_b, own[3])
    lon_a = swap(lon_a, "ox", 0, nx, True)
    lon_b = swap(lon_b, "ox", 1, nx, True)
    wide = 2 * lat
    groups = columns // 8 + 1
    work = [
        pltpu.VMEM((FIELDS, outer, wide), F32),
        pltpu.VMEM((layers, outer, wide), F32),
        pltpu.VMEM((layers, outer, wide), F32),
        pltpu.VMEM((columns + 2 * EDGE, 16, wide), F32),
    ]
    zonal_mid, merid_mid, thick_mid, feat, edge_ext = pl.pallas_call(
        functools.partial(inner_kernel, ny),
        out_shape=[
            flow,
            flow,
            flow,
            jax.ShapeDtypeStruct((groups, PITCH, 256), BF16),
            jax.ShapeDtypeStruct((FIELDS, 48, wide), F32),
        ],
        in_specs=[VMEM] * 15,
        out_specs=[VMEM] * 5,
        scratch_shapes=[
            pltpu.VMEM((7, outer, lat), F32),
            pltpu.VMEM((outer, lat), F32),
            pltpu.VMEM((outer, lat), F32),
            pltpu.VMEM((columns + 2 * EDGE, 16, wide), F32),
        ],
        compiler_params=big,
        cost_estimate=pl.CostEstimate(flops=40_000_000, bytes_accessed=8_000_000, transcendentals=0),
        name="inner",
    )(*inputs, grav, lat_a, lat_b, *own)
    hbm = pl.BlockSpec(memory_space=pltpu.HBM)
    return pl.pallas_call(
        functools.partial(main_kernel, ny),
        out_shape=[flow] * 3 + [jax.ShapeDtypeStruct((columns, lat), F32)],
        in_specs=[VMEM] * 13,
        out_specs=[hbm] * 3 + [VMEM],
        scratch_shapes=work
        + [
            pltpu.VMEM((4, PITCH, 256), BF16),
            pltpu.VMEM((groups, 4, PITCH, 256), BF16),
            pltpu.VMEM((groups, 4, PITCH, 256), BF16),
            pltpu.VMEM((columns // 2 + 1, PITCH, 256), BF16),
            pltpu.VMEM((8 * columns + 16, 128), F32),
            pltpu.VMEM((4 * columns, 128), F32),
            pltpu.VMEM((3, 2, layers, EDGE, lat), F32),
            pltpu.SemaphoreType.DMA((3, 3)),
        ],
        compiler_params=big,
        name="step",
    )(
        zonal_mid,
        merid_mid,
        thick_mid,
        grav,
        lon_a,
        lon_b,
        feat,
        edge_ext,
        w1,
        w2,
        w3,
        b1,
        b2,
    )


def solution(mesh):
    in_specs = (
        P(None, "ox", "oy"),
        P(None, "ox", "oy"),
        P(None, "ox", "oy"),
        P("ox", "oy"),
        P("ox", "oy"),
        P(None, "ox", "oy"),
        P(),
        P(),
        P(),
        P(),
        P(),
        P(),
    )
    out_specs = (P(None, "ox", "oy"), P(None, "ox", "oy"), P(None, "ox", "oy"), P("ox", "oy"))
    body = functools.partial(local, mesh.shape["ox"], mesh.shape["oy"])
    return jax.shard_map(body, mesh=mesh, in_specs=in_specs, out_specs=out_specs, check_vma=False)
```
